128 devices in a mesh: grp: 4 (over z_lo, core), wf: 32 (over x, z_hi, y).
Axes of the slice: x: 4, y: 4, z: 4 (z_hi: 2, z_lo: 2; z = z_hi * 2 + z_lo), core: 2. Of those that a mesh axis runs over, the one named last changes fastest.
Arguments:
- quasi: float32 [128, 4, 262144], P(('grp', 'wf')), may hold values from -6 to 6
- outer_field: float32 [262144], replicated, may hold values from -4 to 4
- coupling: float32 [262144], replicated, may hold values from 2 to 16
Outputs:
- evolved: float32 [128, 4, 262144], P(('grp', 'wf'))
- potentials: float32 [3, 64, 4096], P(None, 'grp', 'wf')
The draws below stay inside these ranges and needn't reach their ends.
All inputs are finite; a program needn't handle non-finite values.
Results may differ from the reference program's by a relative error of at most 0.0003.
Values sent between devices are 32-bit elements; how exact they have to be, the bound alone decides.
A program may use at most 192 MiB of HBM per device.

```python
import math
import jax
import jax.numpy as jnp
from jax import lax

NX = 64
NG = 64
WAVES = 128
CELLS = 262144


def levels(own_key, shape, cuts, low, high):
    gain, own = 1.0, jax.random.fold_in(own_key, 6)
    for axis_at, blocks in cuts:
        steps = jnp.exp(jax.random.uniform(jax.random.fold_in(own, axis_at), (blocks,), jnp.float32, low / len(cuts), high / len(cuts)))
        gain = gain * jnp.repeat(steps, shape[axis_at] // blocks).reshape([-1 if axis == axis_at else 1 for axis in range(len(shape))])
    return gain


def bell_draw(key, shape, deviation, bound, shards=(), kind=jnp.bfloat16):
    drawn = deviation * jax.random.normal(key, shape, jnp.float32)
    if shards:
        drawn = drawn * levels(key, shape, shards, -0.22, 0.18)
    return jnp.clip(drawn, -bound, bound).astype(kind)


def setup_inputs(seed: int = 0) -> dict:
    keys = jax.random.split(jax.random.key(seed), 4)
    quasi = bell_draw(keys[0], (WAVES, 4, CELLS), 1.0, 6.0, ((0, 128),), jnp.float32)
    outer_field = bell_draw(keys[1], (CELLS,), 1.0, 4.0, (), jnp.float32)
    coupling = jnp.clip(jnp.exp(jax.random.uniform(keys[2], (CELLS,), jnp.float32, math.log(2.0), math.log(16.0))), 2.0, 16.0)
    return {"quasi": quasi, "outer_field": outer_field, "coupling": coupling}


time_step = 0.2
kinetic_coef = 0.5
density_coef = 1.0
coulomb_coef = 0.25


def neighbour_sum(field, first, grid):
    positions = jnp.arange(first * grid * grid, dtype=jnp.int32)
    depth_index = positions % grid
    column_index = (positions // grid) % grid
    plane = grid * grid
    total = jnp.roll(field, plane, -1) + jnp.roll(field, -plane, -1)
    total = total + jnp.where(column_index == grid - 1, jnp.roll(field, (grid - 1) * grid, -1), jnp.roll(field, -grid, -1))
    total = total + jnp.where(column_index == 0, jnp.roll(field, -(grid - 1) * grid, -1), jnp.roll(field, grid, -1))
    total = total + jnp.where(depth_index == grid - 1, jnp.roll(field, grid - 1, -1), jnp.roll(field, -1, -1))
    total = total + jnp.where(depth_index == 0, jnp.roll(field, 1 - grid, -1), jnp.roll(field, 1, -1))
    return total - 6.0 * field


def hamiltonian(state, laplace, fields):
    mean_field, pair_real, pair_imag = fields[0], fields[1], fields[2]
    single = -kinetic_coef * laplace + mean_field * state
    first = single[..., 0, :] + pair_real * state[..., 2, :] - pair_imag * state[..., 3, :]
    second = single[..., 1, :] + pair_real * state[..., 3, :] + pair_imag * state[..., 2, :]
    third = pair_real * state[..., 0, :] + pair_imag * state[..., 1, :] - single[..., 2, :]
    fourth = pair_real * state[..., 1, :] - pair_imag * state[..., 0, :] - single[..., 3, :]
    return jnp.stack([first, second, third, fourth], axis=-2)


def propagate(state, laplace, fields, first, grid):
    result = state
    term = state
    for degree in range(1, 5):
        current = laplace if degree == 1 else neighbour_sum(term, first, grid)
        applied = hamiltonian(term, current, fields)
        factor = time_step / degree
        term = jnp.stack([factor * applied[..., 1, :], -factor * applied[..., 0, :],
                          factor * applied[..., 3, :], -factor * applied[..., 2, :]], axis=-2)
        result = result + term
    return result


def lattice_symbol(indices, length):
    return 2.0 - 2.0 * jnp.cos((2.0 * math.pi / length) * indices.astype(jnp.float32))


def reference(quasi, outer_field, coupling):
    def accumulate(carry, state):
        parts = jnp.stack([state[2] * state[2] + state[3] * state[3],
                           state[0] * state[2] + state[1] * state[3],
                           state[1] * state[2] - state[0] * state[3]])
        return carry + parts, None

    summed, unused = lax.scan(accumulate, jnp.zeros((3, CELLS), jnp.float32), quasi)
    summed = summed / WAVES
    symbol_first = lattice_symbol(jnp.arange(NX, dtype=jnp.int32), NX)
    symbol = lattice_symbol(jnp.arange(NG, dtype=jnp.int32), NG)
    squared = symbol_first[:, None, None] + symbol[None, :, None] + symbol[None, None, :]
    kernel = jnp.where(squared > 1e-3, 4.0 * math.pi * coulomb_coef / jnp.where(squared > 1e-3, squared, 1.0), 0.0)
    spectrum = jnp.fft.fftn(summed[0].reshape(NX, NG, NG))
    coulomb = jnp.real(jnp.fft.ifftn(spectrum * kernel)).astype(jnp.float32).reshape(-1)
    fields = jnp.stack([outer_field + density_coef * summed[0] + coulomb,
                        -coupling * summed[1], -coupling * summed[2]])

    def evolve_one(state):
        return propagate(state, neighbour_sum(state, NX, NG), fields, NX, NG)

    evolved = lax.map(evolve_one, quasi)
    return evolved, fields.reshape(3, NX, NG * NG)
```

```python
import math

import jax
import jax.numpy as jnp
import numpy as np
from jax import lax
from jax.experimental import pallas as pl
from jax.experimental.pallas import tpu as pltpu
from jax.sharding import PartitionSpec as P

MESH = pl.DeviceIdType.MESH
N = 64
ROWS = 2048
HALF = 1024
PITCH = 40
PADDED = N * PITCH + 8
GROUP = 8
time_step = 0.2
f32 = jnp.float32
bf16 = jnp.bfloat16

FLOWS = [(0, 0, "xyz"), (0, 1, "yzx"), (1, 0, "zxy"), (1, 1, "xyz"), (2, 0, "yzx"), (2, 1, "zxy")]
PARTS = (128, 32, 8)


def high_low(values):
    high = values.astype(bf16)
    return high, (values - high.astype(f32)).astype(bf16)


def tables():
    index = np.arange(N)
    angle = 2 * math.pi / N * (index[:, None] * index[None, :] % N)
    hartley = (np.cos(angle) + np.sin(angle)) / math.sqrt(N)
    symbol = 2 - 2 * np.cos(2 * math.pi / N * index)
    squared = symbol[:, None, None] + symbol[None, :, None] + symbol[None, None, :]
    spectral = np.where(squared > 0.001, 4 * math.pi * 0.25 / np.maximum(squared, 0.001), 0.0)
    spectral = spectral.reshape(ROWS, 128).astype(np.float32)

    def cut(matrix):
        high = matrix.astype(np.float32).astype(jnp.bfloat16)
        return high, (matrix - high.astype(np.float64)).astype(np.float32).astype(jnp.bfloat16)

    high, low = cut(hartley)
    first = np.concatenate([high, high, low], axis=1)
    blocks = [hartley[p::2, q::2] for p in range(2) for q in range(2)]
    high, low = cut(np.concatenate(blocks, axis=0))
    second = np.concatenate([high, high, low], axis=1)
    third = np.kron(np.eye(2), np.concatenate([hartley, hartley], axis=0))
    third = np.concatenate(cut(third), axis=0)
    lane = np.arange(128)
    near = np.zeros((128, 128), np.float32)
    near[(lane & 64) | ((lane + 1) & 63), lane] += 1
    near[(lane & 64) | ((lane + 63) & 63), lane] += 1
    near = np.concatenate([near, near], axis=0).astype(jnp.bfloat16)
    return first, second, third, spectral, near


def reduce_kernel(q_hbm, full, raw, part, met, got1, got2, got3, in_sem, send_sem, recv_sem):
    grp, wf = lax.axis_index("grp"), lax.axis_index("wf")
    core = grp % 2
    place = {"x": wf // 8, "y": wf % 4, "z": (wf // 4 % 2) * 2 + grp // 2}

    def device(axis, shift):
        at = dict(place)
        at[axis] = (place[axis] + shift) % 4
        return (at["z"] % 2 * 2 + core, at["x"] * 8 + at["z"] // 2 * 4 + at["y"])

    twin = (grp // 2 * 2 + 1 - core, wf)
    chunk = HALF // 2 * 4

    def load(part_index):
        half, side = part_index // 2, part_index % 2
        start = half * 2 * chunk + jnp.where(core == side, chunk, 0)
        rows = pl.ds(pl.multiple_of(start, 8), chunk)
        return pltpu.make_async_copy(q_hbm.at[rows], raw.at[rows], in_sem.at[part_index])

    for index in range(4):
        load(index).start()
    barrier = pltpu.get_barrier_semaphore()
    partners = [twin] + [device(axis, shift) for axis in "xyz" for shift in (1, 2, 3)]
    for partner in partners:
        pl.semaphore_signal(barrier, inc=1, device_id=partner, device_id_type=MESH)

    def send(flow, stage, source, target, to):
        pltpu.make_async_remote_copy(
            src_ref=source, dst_ref=target, send_sem=send_sem.at[flow, stage],
            recv_sem=recv_sem.at[flow, stage], device_id=to, device_id_type=MESH,
        ).start()

    def arrived(flow, stage, rows):
        ref = part.at[0, pl.ds(0, rows)]
        pltpu.make_async_remote_copy(
            src_ref=ref, dst_ref=ref, send_sem=send_sem.at[flow, stage],
            recv_sem=recv_sem.at[flow, stage], device_id=twin, device_id_type=MESH,
        ).wait_recv()

    def sent(flow, stage, rows):
        ref = part.at[0, pl.ds(0, rows)]
        pltpu.make_async_remote_copy(
            src_ref=ref, dst_ref=ref, send_sem=send_sem.at[flow, stage],
            recv_sem=recv_sem.at[flow, stage], device_id=twin, device_id_type=MESH,
        ).wait_send()

    def own(flow, depth):
        field, half, order = FLOWS[flow]
        start = half * HALF + core * 512
        for level in range(depth):
            start = start + place[order[level]] * PARTS[level]
        return start

    for index in range(4):
        half, side = index // 2, index % 2
        load(index).wait()
        begin = half * HALF + jnp.where(core == side, 512, 0)

        @pl.loop(0, 16)
        def partial(step):
            for sub in range(4):
                row = pl.multiple_of(begin + step * 32 + sub * 8, 8)
                a, b, c, d = (raw[pl.ds(row * 4 + k, 8, stride=4), :] for k in range(4))
                part[0, pl.ds(row, 8), :] = c * c + d * d
                part[1, pl.ds(row, 8), :] = a * c + b * d
                part[2, pl.ds(row, 8), :] = b * c - a * d

        if index == 0:
            pl.semaphore_wait(barrier, len(partners))
        if side == 0:
            for flow, (field, flow_half, _) in enumerate(FLOWS):
                if flow_half == half:
                    rows = pl.ds(pl.multiple_of(begin, 8), 512)
                    send(flow, 0, part.at[field, rows], met.at[flow], twin)

    def add_core(flow):
        field = FLOWS[flow][0]
        start = own(flow, 0)
        arrived(flow, 0, 512)

        @pl.loop(0, 8)
        def add(step):
            rows = pl.ds(pl.multiple_of(start + step * 64, 8), 64)
            part[field, rows, :] = part[field, rows, :] + met[flow, pl.ds(step * 64, 64), :]

        scatter(flow, 0)

    def scatter(flow, level):
        field, _, order = FLOWS[flow]
        size = PARTS[level]
        got = (got1, got2, got3)[level]
        for shift in (2, 1, 3):
            peer = (place[order[level]] + shift) % 4
            rows = pl.ds(pl.multiple_of(own(flow, level) + peer * size, 8), size)
            send(flow, 1 + level, part.at[field, rows],
                 got.at[flow, pl.ds((3 - shift) * size, size)], device(order[level], shift))

    def add_axis(flow, level):
        field = FLOWS[flow][0]
        size = PARTS[level]
        got = (got1, got2, got3)[level]
        start = pl.multiple_of(own(flow, level + 1), 8)
        arrived(flow, 1 + level, 3 * size)
        rows = pl.ds(start, size)
        total = part[field, rows, :]
        for slot in range(3):
            total = total + got[flow, pl.ds(slot * size, size), :]
        if level < 2:
            part[field, rows, :] = total
            scatter(flow, level + 1)
        else:
            full[field, rows, :] = total * (1.0 / 128.0)
            spread(flow, 2)

    def spread(flow, level):
        field, _, order = FLOWS[flow]
        rows = pl.ds(pl.multiple_of(own(flow, level + 1), 8), PARTS[level])
        for shift in (2, 1, 3):
            send(flow, 6 - level, full.at[field, rows], full.at[field, rows],
                 device(order[level], shift))

    def gathered(flow, level):
        arrived(flow, 6 - level, 3 * PARTS[level])
        if level > 0:
            spread(flow, level - 1)
        else:
            field = FLOWS[flow][0]
            rows = pl.ds(pl.multiple_of(own(flow, 0), 8), 512)
            send(flow, 7, full.at[field, rows], full.at[field, rows], twin)

    first, rest = (0, 1), (2, 3, 4, 5)

    def each(flows, call, *levels):
        for flow in flows:
            call(flow, *levels)

    each(first, add_core)
    each(rest, add_core)
    each(first, add_axis, 0)
    each(first, add_axis, 1)
    each(rest, add_axis, 0)
    each(first, add_axis, 2)
    each(rest, add_axis, 1)
    each(first, gathered, 2)
    each(rest, add_axis, 2)
    each(first, gathered, 1)
    each(rest, gathered, 2)
    each(first, gathered, 0)
    each(rest, gathered, 1)
    each(rest, gathered, 0)
    each(first + rest, lambda flow: arrived(flow, 7, 512))
    for flow in first + rest:
        for stage, rows in enumerate((512, 384, 96, 24, 24, 96, 384, 512)):
            sent(flow, stage, rows)


def evolve_kernel(q_hbm, sums_hbm, outer_hbm, coupling_hbm, first, second, third, spectral, near,
                  out_hbm, potentials, raw, sums, outer, coupling, work, hill, fields,
                  start, ping, pong, beside, in_sem, field_sem, out_sem):
    chunks = 8
    size = 8192 // chunks
    copies = [pltpu.make_async_copy(sums_hbm.at[field], sums.at[field], field_sem.at[field]) for field in range(3)]
    copies.append(pltpu.make_async_copy(outer_hbm, outer, field_sem.at[3]))
    copies.append(pltpu.make_async_copy(coupling_hbm, coupling, field_sem.at[4]))
    for copy in copies:
        copy.start()

    def load(index):
        rows = pl.ds(index * size, size)
        return pltpu.make_async_copy(q_hbm.at[rows], raw.at[rows], in_sem.at[index])

    def save(index):
        rows = pl.ds(index * size, size)
        return pltpu.make_async_copy(raw.at[rows], out_hbm.at[rows], out_sem.at[index])

    for index in range(chunks):
        load(index).start()

    def thrice(values):
        high, low = high_low(values)
        return jnp.concatenate([high, low, high], axis=0)

    def along_first(source, target):
        @pl.loop(0, 8)
        def columns(step):
            slices = [pl.ds(step * 4 + k, N, stride=32) for k in range(4)]
            values = jnp.concatenate([source[s, :] for s in slices], axis=1)
            result = jnp.dot(first[...], thrice(values), preferred_element_type=f32)
            for k in range(4):
                target[slices[k], :] = result[:, 128 * k:128 * k + 128]

    def along_rest(source, target, weigh):
        low_lanes = lax.broadcasted_iota(jnp.int32, (32, 128), 1) < 64

        @pl.loop(0, 8)
        def planes(step):
            base = pl.multiple_of(step * 256, 256)
            values = jnp.concatenate([source[pl.ds(base + 32 * k, 32), :] for k in range(8)], axis=1)
            mixed = jnp.dot(second[...], thrice(values), preferred_element_type=f32)
            parts = []
            for k in range(8):
                piece = mixed[:, 128 * k:128 * k + 128]
                parts.append(jnp.concatenate([
                    jnp.where(low_lanes, piece[0:32], piece[32:64]),
                    jnp.where(low_lanes, piece[64:96], piece[96:128])], axis=1))
            high, low = high_low(jnp.concatenate(parts, axis=0))
            result = jnp.dot(high, third[0:256, :], preferred_element_type=f32)
            result = result + jnp.dot(low, third[0:256, :], preferred_element_type=f32)
            result = result + jnp.dot(high, third[256:512, :], preferred_element_type=f32)
            if weigh:
                result = result * spectral[pl.ds(base, 256), :]
            target[pl.ds(base, 256), :] = result

    copies[0].wait()
    along_first(sums.at[0], work)
    along_rest(work, hill, True)
    along_rest(hill, work, False)
    along_first(work, hill)

    def put(state, component, plane, block, values):
        base = plane * PITCH + 8
        state[component, pl.ds(base + 8 * block, 8), :] = values
        if block == 0:
            state[component, pl.ds(base + 32, 1), :] = values[0:1]
        if block == 3:
            state[component, pl.ds(base - 1, 1), :] = values[7:8]

    for index in range(chunks):
        load(index).wait()

        @pl.loop(index * (N // chunks), (index + 1) * (N // chunks))
        def planes(plane):
            for component in range(4):
                for block in range(4):
                    put(start, component, plane, block,
                        raw[pl.ds(plane * 128 + block * 32 + component, 8, stride=4), :])

    for copy in copies[1:]:
        copy.wait()

    @pl.loop(0, 64)
    def fill(step):
        for sub in range(4):
            rows = pl.ds(pl.multiple_of(step * 32 + sub * 8, 8), 8)
            mean = outer[rows, :] + sums[0, rows, :] + hill[rows, :]
            scale = -2.0 * coupling[rows, :]
            fields[0, rows, :] = 2.0 * mean + 6.0
            fields[1, rows, :] = scale * sums[1, rows, :]
            fields[2, rows, :] = scale * sums[2, rows, :]

    held = pl.ds(lax.axis_index("grp") * 512 + lax.axis_index("wf"), 16, stride=32)
    potentials[0] = outer[held, :] + sums[0, held, :] + hill[held, :]
    potentials[1] = -coupling[held, :] * sums[1, held, :]
    potentials[2] = -coupling[held, :] * sums[2, held, :]

    upper = lax.broadcasted_iota(jnp.int32, (8, 128), 1) >= 64

    def step(source, factor, store):
        def group(index):
            plane0 = index * GROUP
            lines = []
            for sub in range(GROUP):
                for component in range(4):
                    values = source[component, pl.ds((plane0 + sub) * PITCH + 8, 32), :]
                    lines.append(jnp.concatenate(high_low(values), axis=1))
            beside[...] = jnp.dot(jnp.concatenate(lines, axis=0), near[...], preferred_element_type=f32)
            for sub in range(GROUP):
                plane = plane0 + sub
                base = plane * PITCH + 8
                before = lax.rem(plane + N - 1, N) * PITCH + 8
                after = lax.rem(plane + 1, N) * PITCH + 8
                for block in range(4):
                    row = 8 * block
                    state, total = [], []
                    for component in range(4):
                        here = source[component, pl.ds(base + row, 8), :]
                        up = source[component, pl.ds(base + row - 1, 8), :]
                        down = source[component, pl.ds(base + row + 1, 8), :]
                        across = pltpu.roll(here + jnp.where(upper, up, down), 64, 1)
                        along = source[component, pl.ds(before + row, 8), :] + source[component, pl.ds(after + row, 8), :]
                        total.append(beside[pl.ds((sub * 4 + component) * 32 + row, 8), :] + along + across)
                        state.append(here)
                    rows = pl.ds(pl.multiple_of(plane * 32, 32) + row, 8)
                    mean, real, imag = fields[0, rows, :], fields[1, rows, :], fields[2, rows, :]
                    a, b, c, d = state
                    made = [mean * a - total[0] + (real * c - imag * d),
                            mean * b - total[1] + (real * d + imag * c),
                            (real * a + imag * b) - (mean * c - total[2]),
                            (real * b - imag * a) - (mean * d - total[3])]
                    old = [start[component, pl.ds(base + row, 8), :] for component in range(4)]
                    half = 0.5 * factor
                    store(plane, block, [old[0] + half * made[1], old[1] - half * made[0],
                                         old[2] + half * made[3], old[3] - half * made[2]])
        return group

    def into(state):
        def store(plane, block, values):
            for component in range(4):
                put(state, component, plane, block, values[component])
        return store

    def finish(plane, block, values):
        for component in range(4):
            raw[pl.ds(plane * 128 + block * 32 + component, 8, stride=4), :] = values[component]

    for source, degree, target in ((start, 4, ping), (ping, 3, pong), (pong, 2, ping)):
        pl.loop(0, N // GROUP)(step(source, time_step / degree, into(target)))
    last = step(ping, time_step, finish)

    @pl.loop(0, chunks)
    def groups(index):
        last(index)
        save(index).start()

    for index in range(chunks):
        save(index).wait()


def local(quasi, outer_field, coupling):
    rows = quasi.reshape(4, ROWS, 128).transpose(1, 0, 2).reshape(4 * ROWS, 128)
    anywhere = pl.BlockSpec(memory_space=pl.ANY)
    inside = pl.BlockSpec(memory_space=pltpu.VMEM)
    sums = pl.pallas_call(
        reduce_kernel,
        out_shape=jax.ShapeDtypeStruct((3, ROWS, 128), f32),
        in_specs=[anywhere],
        out_specs=inside,
        scratch_shapes=[
            pltpu.VMEM((4 * ROWS, 128), f32),
            pltpu.VMEM((3, ROWS, 128), f32),
            pltpu.VMEM((6, 512, 128), f32),
            pltpu.VMEM((6, 384, 128), f32),
            pltpu.VMEM((6, 96, 128), f32),
            pltpu.VMEM((6, 24, 128), f32),
            pltpu.SemaphoreType.DMA((4,)),
            pltpu.SemaphoreType.DMA((6, 8)),
            pltpu.SemaphoreType.DMA((6, 8)),
        ],
        compiler_params=pltpu.CompilerParams(
            collective_id=0, has_side_effects=True, vmem_limit_bytes=40 * 2**20),
        name="reduce",
    )(rows)
    weights = tables()
    evolved, potentials = pl.pallas_call(
        evolve_kernel,
        out_shape=(jax.ShapeDtypeStruct((4 * ROWS, 128), f32), jax.ShapeDtypeStruct((3, 16, 128), f32)),
        in_specs=[anywhere] * 4 + [inside] * 5,
        out_specs=(anywhere, inside),
        scratch_shapes=[
            pltpu.VMEM((4 * ROWS, 128), f32),
            pltpu.VMEM((3, ROWS, 128), f32),
            pltpu.VMEM((ROWS, 128), f32),
            pltpu.VMEM((ROWS, 128), f32),
            pltpu.VMEM((ROWS, 128), f32),
            pltpu.VMEM((ROWS, 128), f32),
            pltpu.VMEM((3, ROWS, 128), f32),
            pltpu.VMEM((4, PADDED, 128), f32),
            pltpu.VMEM((4, PADDED, 128), f32),
            pltpu.VMEM((4, PADDED, 128), f32),
            pltpu.VMEM((GROUP * 128, 128), f32),
            pltpu.SemaphoreType.DMA((8,)),
            pltpu.SemaphoreType.DMA((5,)),
            pltpu.SemaphoreType.DMA((8,)),
        ],
        compiler_params=pltpu.CompilerParams(vmem_limit_bytes=56 * 2**20),
        name="evolve",
    )(rows, sums, outer_field.reshape(ROWS, 128), coupling.reshape(ROWS, 128), *[jnp.asarray(w) for w in weights])
    evolved = evolved.reshape(ROWS, 4, 128).transpose(1, 0, 2).reshape(1, 4, ROWS * 128)
    return evolved, potentials


def solution(mesh):
    return jax.shard_map(
        local,
        mesh=mesh,
        in_specs=(P(("grp", "wf"), None, None), P(), P()),
        out_specs=(P(("grp", "wf"), None, None), P(None, "grp", "wf")),
        check_vma=False,
    )
```

```python
import math

import jax
import jax.numpy as jnp
import numpy as np
from jax import lax
from jax.experimental import pallas as pl
from jax.experimental.pallas import tpu as pltpu
from jax.sharding import PartitionSpec as P

MESH = pl.DeviceIdType.MESH
N = 64
ROWS = 2048
HALF = 1024
PITCH = 40
PADDED = N * PITCH + 8
GROUP = 8
VMEM_MIB = 58
time_step = 0.2
f32 = jnp.float32
bf16 = jnp.bfloat16

FLOWS = [(0, 0, "xyz"), (0, 1, "yzx"), (1, 0, "zxy"), (1, 1, "xyz"), (2, 0, "yzx"), (2, 1, "zxy")]
PARTS = (128, 32, 8)


def high_low(values):
    high = values.astype(bf16)
    return high, (values - high.astype(f32)).astype(bf16)


def tables():
    index = np.arange(N)
    angle = 2 * math.pi / N * (index[:, None] * index[None, :] % N)
    hartley = (np.cos(angle) + np.sin(angle)) / math.sqrt(N)
    symbol = 2 - 2 * np.cos(2 * math.pi / N * index)
    squared = symbol[:, None, None] + symbol[None, :, None] + symbol[None, None, :]
    spectral = np.where(squared > 0.001, 4 * math.pi * 0.25 / np.maximum(squared, 0.001), 0.0)
    spectral = spectral.reshape(ROWS, 128).astype(np.float32)

    def cut(matrix):
        high = matrix.astype(np.float32).astype(jnp.bfloat16)
        return high, (matrix - high.astype(np.float64)).astype(np.float32).astype(jnp.bfloat16)

    high, low = cut(hartley)
    first = np.concatenate([high, high, low], axis=1)
    blocks = [hartley[p::2, q::2] for p in range(2) for q in range(2)]
    high, low = cut(np.concatenate(blocks, axis=0))
    second = np.concatenate([high, high, low], axis=1)
    third = np.kron(np.eye(2), np.concatenate([hartley, hartley], axis=0))
    third = np.concatenate(cut(third), axis=0)
    lane = np.arange(128)
    near = np.zeros((128, 128), np.float32)
    near[(lane & 64) | ((lane + 1) & 63), lane] += 1
    near[(lane & 64) | ((lane + 63) & 63), lane] += 1
    near = np.concatenate([near, near], axis=0).astype(jnp.bfloat16)
    return first, second, third, spectral, near


def put(state, component, plane, block, values):
    base = plane * PITCH + 8
    state[component, pl.ds(base + 8 * block, 8), :] = values
    if block == 0:
        state[component, pl.ds(base + 32, 1), :] = values[0:1]
    if block == 3:
        state[component, pl.ds(base - 1, 1), :] = values[7:8]


def beside_planes(source, near, beside, plane0):
    lines = []
    for sub in range(GROUP):
        for component in range(4):
            values = source[component, pl.ds((plane0 + sub) * PITCH + 8, 32), :]
            lines.append(jnp.concatenate(high_low(values), axis=1))
    beside[...] = jnp.dot(jnp.concatenate(lines, axis=0), near[...], preferred_element_type=f32)


def neighbours(source, beside, upper, plane, sub, component, row):
    base = plane * PITCH + 8
    before = lax.rem(plane + N - 1, N) * PITCH + 8
    after = lax.rem(plane + 1, N) * PITCH + 8
    here = source[component, pl.ds(base + row, 8), :]
    up = source[component, pl.ds(base + row - 1, 8), :]
    down = source[component, pl.ds(base + row + 1, 8), :]
    across = pltpu.roll(here + jnp.where(upper, up, down), 64, 1)
    along = source[component, pl.ds(before + row, 8), :] + source[component, pl.ds(after + row, 8), :]
    return here, beside[pl.ds((sub * 4 + component) * 32 + row, 8), :] + along + across


def kernel(q_hbm, outer_hbm, coupling_hbm, first_hbm, second_hbm, third_hbm, spectral_hbm, near_hbm,
           out_hbm, potentials, raw, fields, start, laplace, ping, pong, part, full, met, got1, got2, got3,
           outer, coupling, first, second, third, spectral, near, work, hill, beside,
           in_sem, send_sem, recv_sem, side_sem, out_sem):
    grp, wf = lax.axis_index("grp"), lax.axis_index("wf")
    core = grp % 2
    place = {"x": wf // 8, "y": wf % 4, "z": (wf // 4 % 2) * 2 + grp // 2}

    def device(axis, shift):
        at = dict(place)
        at[axis] = (place[axis] + shift) % 4
        return (at["z"] % 2 * 2 + core, at["x"] * 8 + at["z"] // 2 * 4 + at["y"])

    twin = (grp // 2 * 2 + 1 - core, wf)
    pieces = ((0, 0), (1, 0), (0, 1), (1, 1))

    def begin_of(piece):
        half, side = pieces[piece]
        return half * HALF + jnp.where(core == side, 512, 0)

    def load(piece):
        rows = pl.ds(pl.multiple_of(begin_of(piece) * 4, 8), 2048)
        return pltpu.make_async_copy(q_hbm.at[rows], raw.at[rows], in_sem.at[piece])

    for piece in range(4):
        load(piece).start()
    barrier = pltpu.get_barrier_semaphore()
    partners = [twin] + [device(axis, shift) for axis in "xyz" for shift in (1, 2, 3)]
    for partner in partners:
        pl.semaphore_signal(barrier, inc=1, device_id=partner, device_id_type=MESH)
    tables_in = [
        pltpu.make_async_copy(source, target, side_sem.at[index])
        for index, (source, target) in enumerate((
            (near_hbm, near), (first_hbm, first), (second_hbm, second), (third_hbm, third),
            (spectral_hbm, spectral), (outer_hbm, outer), (coupling_hbm, coupling)))
    ]
    for copy in tables_in:
        copy.start()

    def send(flow, stage, source, target, to):
        pltpu.make_async_remote_copy(
            src_ref=source, dst_ref=target, send_sem=send_sem.at[flow, stage],
            recv_sem=recv_sem.at[flow, stage], device_id=to, device_id_type=MESH,
        ).start()

    def whole(flow, stage, rows):
        ref = part.at[0, pl.ds(0, rows)]
        return pltpu.make_async_remote_copy(
            src_ref=ref, dst_ref=ref, send_sem=send_sem.at[flow, stage],
            recv_sem=recv_sem.at[flow, stage], device_id=twin, device_id_type=MESH,
        )

    def arrived(flow, stage, rows):
        whole(flow, stage, rows).wait_recv()

    def own(flow, depth):
        field, half, order = FLOWS[flow]
        begin = half * HALF + core * 512
        for level in range(depth):
            begin = begin + place[order[level]] * PARTS[level]
        return begin

    def partial(piece):
        half, side = pieces[piece]
        begin = begin_of(piece)
        load(piece).wait()

        @pl.loop(0, 8)
        def rows_of(step):
            for sub in range(8):
                row = pl.multiple_of(begin + step * 64 + sub * 8, 8)
                a, b, c, d = (raw[pl.ds(row * 4 + k, 8, stride=4), :] for k in range(4))
                part[0, pl.ds(row, 8), :] = c * c + d * d
                part[1, pl.ds(row, 8), :] = a * c + b * d
                part[2, pl.ds(row, 8), :] = b * c - a * d

        if piece == 0:
            pl.semaphore_wait(barrier, len(partners))
        if side == 0:
            for flow, (field, flow_half, _) in enumerate(FLOWS):
                if flow_half == half:
                    rows = pl.ds(pl.multiple_of(begin, 8), 512)
                    send(flow, 0, part.at[field, rows], met.at[flow], twin)

    def add_core(flow):
        field = FLOWS[flow][0]
        begin = own(flow, 0)
        arrived(flow, 0, 512)

        @pl.loop(0, 4)
        def add(step):
            rows = pl.ds(pl.multiple_of(begin + step * 128, 8), 128)
            part[field, rows, :] = part[field, rows, :] + met[flow, pl.ds(step * 128, 128), :]

        scatter(flow, 0)

    def scatter(flow, level):
        field, _, order = FLOWS[flow]
        size = PARTS[level]
        got = (got1, got2, got3)[level]
        for shift in (2, 1, 3):
            peer = (place[order[level]] + shift) % 4
            rows = pl.ds(pl.multiple_of(own(flow, level) + peer * size, 8), size)
            send(flow, 1 + level, part.at[field, rows],
                 got.at[flow, pl.ds((3 - shift) * size, size)], device(order[level], shift))

    def add_axis(flow, level):
        field = FLOWS[flow][0]
        size = PARTS[level]
        got = (got1, got2, got3)[level]
        begin = pl.multiple_of(own(flow, level + 1), 8)
        arrived(flow, 1 + level, 3 * size)
        rows = pl.ds(begin, size)
        total = part[field, rows, :]
        for slot in range(3):
            total = total + got[flow, pl.ds(slot * size, size), :]
        if level < 2:
            part[field, rows, :] = total
            scatter(flow, level + 1)
        else:
            full[field, rows, :] = total * (1.0 / 128.0)
            spread(flow, 2)

    def spread(flow, level):
        field, _, order = FLOWS[flow]
        rows = pl.ds(pl.multiple_of(own(flow, level + 1), 8), PARTS[level])
        for shift in (2, 1, 3):
            send(flow, 6 - level, full.at[field, rows], full.at[field, rows],
                 device(order[level], shift))

    def gathered(flow, level):
        arrived(flow, 6 - level, 3 * PARTS[level])
        if level > 0:
            spread(flow, level - 1)
        else:
            field = FLOWS[flow][0]
            rows = pl.ds(pl.multiple_of(own(flow, 0), 8), 512)
            send(flow, 7, full.at[field, rows], full.at[field, rows], twin)

    def thrice(values):
        high, low = high_low(values)
        return jnp.concatenate([high, low, high], axis=0)

    def along_first(source, target, level):
        @pl.loop(0, 2)
        def columns(group):
            for sub in range(4):
                step = group * 4 + sub
                slices = [pl.ds(step * 4 + k, N, stride=32) for k in range(4)]
                values = jnp.concatenate([source[s, :] for s in slices], axis=1)
                if level is not None:
                    values = values - level
                result = jnp.dot(first[...], thrice(values), preferred_element_type=f32)
                for k in range(4):
                    target[slices[k], :] = result[:, 128 * k:128 * k + 128]

    def along_rest(source, target, weigh):
        low_lanes = lax.broadcasted_iota(jnp.int32, (32, 128), 1) < 64

        @pl.loop(0, 2)
        def planes(group):
            for sub in range(4):
                base = pl.multiple_of((group * 4 + sub) * 256, 256)
                values = jnp.concatenate([source[pl.ds(base + 32 * k, 32), :] for k in range(8)], axis=1)
                mixed = jnp.dot(second[...], thrice(values), preferred_element_type=f32)
                parts = []
                for k in range(8):
                    piece = mixed[:, 128 * k:128 * k + 128]
                    parts.append(jnp.concatenate([
                        jnp.where(low_lanes, piece[0:32], piece[32:64]),
                        jnp.where(low_lanes, piece[64:96], piece[96:128])], axis=1))
                high, low = high_low(jnp.concatenate(parts, axis=0))
                result = jnp.dot(high, third[0:256, :], preferred_element_type=f32)
                result = result + jnp.dot(low, third[0:256, :], preferred_element_type=f32)
                result = result + jnp.dot(high, third[256:512, :], preferred_element_type=f32)
                if weigh:
                    result = result * spectral[pl.ds(base, 256), :]
                target[pl.ds(base, 256), :] = result

    def prepare():
        @pl.loop(0, 32)
        def planes(pair):
            for plane in (pair * 2, pair * 2 + 1):
                for component in range(4):
                    for block in range(4):
                        put(start, component, plane, block,
                            raw[pl.ds(plane * 128 + block * 32 + component, 8, stride=4), :])

        tables_in[0].wait()
        upper = lax.broadcasted_iota(jnp.int32, (8, 128), 1) >= 64

        @pl.loop(0, N // GROUP)
        def groups(index):
            plane0 = index * GROUP
            beside_planes(start, near, beside, plane0)
            for sub in range(GROUP):
                plane = plane0 + sub
                for block in range(4):
                    rows = pl.ds(pl.multiple_of(plane * 32, 32) + 8 * block, 8)
                    for component in range(4):
                        laplace[component, rows, :] = neighbours(
                            start, beside, upper, plane, sub, component, 8 * block)[1]

    lead, rest = (0, 1), (2, 3, 4, 5)

    def each(flows, call, *levels):
        for flow in flows:
            call(flow, *levels)

    partial(0)
    partial(1)
    partial(2)
    add_core(0)
    partial(3)
    add_core(1)
    each(rest, add_core)
    prepare()
    each(lead, add_axis, 0)
    each(lead, add_axis, 1)
    each(rest, add_axis, 0)
    each(lead, add_axis, 2)
    each(rest, add_axis, 1)
    each(lead, gathered, 2)
    each(rest, add_axis, 2)
    each(lead, gathered, 1)
    each(rest, gathered, 2)
    each(lead, gathered, 0)
    each(rest, gathered, 1)
    for copy in tables_in[1:]:
        copy.wait()
    each(lead, lambda flow: arrived(flow, 7, 512))
    total = full[0, 0:64, :]
    for index in range(1, 32):
        total = total + full[0, 64 * index:64 * index + 64, :]
    along_first(full.at[0], work, jnp.sum(total) * (1.0 / (ROWS * 128)))
    along_rest(work, hill, True)
    each(rest, gathered, 0)
    along_rest(hill, work, False)
    along_first(work, hill, None)
    each(rest, lambda flow: arrived(flow, 7, 512))

    @pl.loop(0, 32)
    def fill(step):
        for sub in range(8):
            rows = pl.ds(pl.multiple_of(step * 64 + sub * 8, 8), 8)
            scale = -2.0 * coupling[rows, :]
            fields[0, rows, :] = 2.0 * (outer[rows, :] + full[0, rows, :] + hill[rows, :]) + 6.0
            fields[1, rows, :] = scale * full[1, rows, :]
            fields[2, rows, :] = scale * full[2, rows, :]

    held = pl.ds(lax.axis_index("grp") * 512 + lax.axis_index("wf"), 16, stride=32)
    potentials[0] = 0.5 * fields[0, held, :] - 3.0
    potentials[1] = 0.5 * fields[1, held, :]
    potentials[2] = 0.5 * fields[2, held, :]
    upper = lax.broadcasted_iota(jnp.int32, (8, 128), 1) >= 64

    def combine(plane, block, state, total, factor, store):
        rows = pl.ds(pl.multiple_of(plane * 32, 32) + 8 * block, 8)
        mean, real, imag = fields[0, rows, :], fields[1, rows, :], fields[2, rows, :]
        a, b, c, d = state
        made = [mean * a - total[0] + (real * c - imag * d),
                mean * b - total[1] + (real * d + imag * c),
                (real * a + imag * b) - (mean * c - total[2]),
                (real * b - imag * a) - (mean * d - total[3])]
        old = [start[component, pl.ds(plane * PITCH + 8 + 8 * block, 8), :] for component in range(4)]
        half = 0.5 * factor
        store(plane, block, [old[0] + half * made[1], old[1] - half * made[0],
                             old[2] + half * made[3], old[3] - half * made[2]])

    def step(source, factor, store):
        def group(index):
            plane0 = index * GROUP
            beside_planes(source, near, beside, plane0)
            for sub in range(GROUP):
                for block in range(4):
                    both = [neighbours(source, beside, upper, plane0 + sub, sub, component, 8 * block)
                            for component in range(4)]
                    combine(plane0 + sub, block, [b[0] for b in both], [b[1] for b in both], factor, store)
        return group

    def into(state):
        def store(plane, block, values):
            for component in range(4):
                put(state, component, plane, block, values[component])
        return store

    def finish(plane, block, values):
        for component in range(4):
            raw[pl.ds(plane * 128 + block * 32 + component, 8, stride=4), :] = values[component]

    @pl.loop(0, N // 4)
    def opening(index):
        for sub in range(4):
            plane = index * 4 + sub
            for block in range(4):
                rows = pl.ds(pl.multiple_of(plane * 32, 32) + 8 * block, 8)
                state = [start[component, pl.ds(plane * PITCH + 8 + 8 * block, 8), :] for component in range(4)]
                total = [laplace[component, rows, :] for component in range(4)]
                combine(plane, block, state, total, time_step / 4, into(ping))

    for source, degree, target in ((ping, 3, pong), (pong, 2, ping)):
        pl.loop(0, N // GROUP)(step(source, time_step / degree, into(target)))
    last = step(ping, time_step, finish)

    def save(index):
        rows = pl.ds(index * 1024, 1024)
        return pltpu.make_async_copy(raw.at[rows], out_hbm.at[rows], out_sem.at[index])

    @pl.loop(0, N // GROUP)
    def closing(index):
        last(index)
        save(index).start()

    for index in range(N // GROUP):
        save(index).wait()
    for flow in lead + rest:
        for stage, rows in enumerate((512, 384, 96, 24, 24, 96, 384, 512)):
            whole(flow, stage, rows).wait_send()


def local(quasi, outer_field, coupling):
    rows = quasi.reshape(4, ROWS, 128).transpose(1, 0, 2).reshape(4 * ROWS, 128)
    far = pl.BlockSpec(memory_space=pltpu.HBM)
    inside = pl.BlockSpec(memory_space=pltpu.VMEM)
    weights = [jnp.asarray(w) for w in tables()]
    shape = jax.ShapeDtypeStruct
    state = pltpu.VMEM((4, PADDED, 128), f32)
    field = pltpu.VMEM((ROWS, 128), f32)
    evolved, potentials = pl.pallas_call(
        kernel,
        out_shape=(shape((4 * ROWS, 128), f32), shape((3, 16, 128), f32)),
        in_specs=[far] * 8,
        out_specs=(far, inside),
        scratch_shapes=[
            pltpu.VMEM((4 * ROWS, 128), f32),
            pltpu.VMEM((3, ROWS, 128), f32),
            state,
            pltpu.VMEM((4, ROWS, 128), f32),
            state,
            state,
            pltpu.VMEM((3, ROWS, 128), f32),
            pltpu.VMEM((3, ROWS, 128), f32),
            pltpu.VMEM((6, 512, 128), f32),
            pltpu.VMEM((6, 384, 128), f32),
            pltpu.VMEM((6, 96, 128), f32),
            pltpu.VMEM((6, 24, 128), f32),
            field,
            field,
        ] + [pltpu.VMEM(w.shape, w.dtype) for w in weights] + [
            field,
            field,
            pltpu.VMEM((GROUP * 128, 128), f32),
            pltpu.SemaphoreType.DMA((4,)),
            pltpu.SemaphoreType.DMA((6, 8)),
            pltpu.SemaphoreType.DMA((6, 8)),
            pltpu.SemaphoreType.DMA((7,)),
            pltpu.SemaphoreType.DMA((N // GROUP,)),
        ],
        compiler_params=pltpu.CompilerParams(
            collective_id=0, has_side_effects=True, vmem_limit_bytes=VMEM_MIB * 2**20),
        name="superfluid",
    )(rows, outer_field.reshape(ROWS, 128), coupling.reshape(ROWS, 128), *weights)
    evolved = evolved.reshape(ROWS, 4, 128).transpose(1, 0, 2).reshape(1, 4, ROWS * 128)
    return evolved, potentials


def solution(mesh):
    return jax.shard_map(
        local,
        mesh=mesh,
        in_specs=(P(("grp", "wf"), None, None), P(), P()),
        out_specs=(P(("grp", "wf"), None, None), P(None, "grp", "wf")),
        check_vma=False,
    )
```

```python
import math

import jax
import jax.numpy as jnp
import numpy as np
from jax import lax
from jax.experimental import pallas as pl
from jax.experimental.pallas import tpu as pltpu
from jax.sharding import PartitionSpec as P

MESH = pl.DeviceIdType.MESH
N = 64
ROWS = 2048
HALF = 1024
PITCH = 40
PADDED = N * PITCH + 8
GROUP = 8
VMEM_MIB = 58
time_step = 0.2
f32 = jnp.float32
bf16 = jnp.bfloat16

FLOWS = [(0, 0, "xyz"), (0, 1, "yzx"), (1, 0, "zxy"), (1, 1, "xyz"), (2, 0, "yzx"), (2, 1, "zxy")]
PARTS = (128, 32, 8)


def high_low(values):
    high = values.astype(bf16)
    return high, (values - high.astype(f32)).astype(bf16)


def tables():
    index = np.arange(N)
    angle = 2 * math.pi / N * (index[:, None] * index[None, :] % N)
    hartley = (np.cos(angle) + np.sin(angle)) / math.sqrt(N)
    symbol = 2 - 2 * np.cos(2 * math.pi / N * index)
    squared = symbol[:, None, None] + symbol[None, :, None] + symbol[None, None, :]
    spectral = np.where(squared > 0.001, 4 * math.pi * 0.25 / np.maximum(squared, 0.001), 0.0)
    spectral = spectral.reshape(ROWS, 128).astype(np.float32)

    def cut(matrix):
        high = matrix.astype(np.float32).astype(jnp.bfloat16)
        return high, (matrix - high.astype(np.float64)).astype(np.float32).astype(jnp.bfloat16)

    high, low = cut(hartley)
    first = np.concatenate([high, high, low], axis=1)
    high, low = cut(np.concatenate([
        np.concatenate([hartley[q::2, p::2] for p in range(2)], axis=1) for q in range(2)], axis=0))
    second = np.concatenate([high, high, low], axis=1)
    third = np.concatenate(cut(np.kron(np.eye(2), np.concatenate([hartley, hartley], axis=0))), axis=1)
    lane = np.arange(128)
    near = np.zeros((128, 128), np.float32)
    near[(lane & 64) | ((lane + 1) & 63), lane] += 1
    near[(lane & 64) | ((lane + 63) & 63), lane] += 1
    near = np.concatenate([near, near], axis=0).astype(jnp.bfloat16)
    return first, second, third, spectral, near


def put(state, component, plane, block, values):
    base = plane * PITCH + 8
    state[component, pl.ds(base + 8 * block, 8), :] = values
    if block == 0:
        state[component, pl.ds(base + 32, 1), :] = values[0:1]
    if block == 3:
        state[component, pl.ds(base - 1, 1), :] = values[7:8]


def beside_planes(source, near, beside, plane0):
    lines = []
    for sub in range(GROUP):
        for component in range(4):
            values = source[component, pl.ds((plane0 + sub) * PITCH + 8, 32), :]
            lines.append(jnp.concatenate(high_low(values), axis=1))
    beside[...] = jnp.dot(jnp.concatenate(lines, axis=0), near[...], preferred_element_type=f32)


def neighbours(source, beside, upper, plane, sub, component, row):
    base = plane * PITCH + 8
    before = lax.rem(plane + N - 1, N) * PITCH + 8
    after = lax.rem(plane + 1, N) * PITCH + 8
    here = source[component, pl.ds(base + row, 8), :]
    up = source[component, pl.ds(base + row - 1, 8), :]
    down = source[component, pl.ds(base + row + 1, 8), :]
    across = pltpu.roll(here + jnp.where(upper, up, down), 64, 1)
    along = source[component, pl.ds(before + row, 8), :] + source[component, pl.ds(after + row, 8), :]
    return here, beside[pl.ds((sub * 4 + component) * 32 + row, 8), :] + along + across


def kernel(q_hbm, outer_hbm, coupling_hbm, first_hbm, second_hbm, third_hbm, spectral_hbm, near_hbm,
           out_hbm, potentials, raw, fields, start, laplace, ping, pong, part, full, met, got1, got2,
           outer, coupling, first, second, third, spectral, near, work, hill, beside,
           in_sem, send_sem, recv_sem, side_sem, out_sem):
    grp, wf = lax.axis_index("grp"), lax.axis_index("wf")
    core = grp % 2
    place = {"x": wf // 8, "y": wf % 4, "z": (wf // 4 % 2) * 2 + grp // 2}

    def device(axis, shift, also=None, by=0):
        at = dict(place)
        at[axis] = (place[axis] + shift) % 4
        if also:
            at[also] = (place[also] + by) % 4
        return (at["z"] % 2 * 2 + core, at["x"] * 8 + at["z"] // 2 * 4 + at["y"])

    twin = (grp // 2 * 2 + 1 - core, wf)
    pieces = ((0, 0), (1, 0), (0, 1), (1, 1))

    def begin_of(piece):
        half, side = pieces[piece]
        return half * HALF + jnp.where(core == side, 512, 0)

    def load(piece):
        rows = pl.ds(pl.multiple_of(begin_of(piece) * 4, 8), 2048)
        return pltpu.make_async_copy(q_hbm.at[rows], raw.at[rows], in_sem.at[piece])

    barrier = pltpu.get_barrier_semaphore()
    partners = [device(axes[0], shift, axes[1], by) for axes in ("xy", "yz", "zx") for shift in (2, 1, 3) for by in (2, 1, 3)]
    partners += [device(axis, shift) for axis in "xyz" for shift in (2, 1, 3)] + [twin]
    for partner in partners:
        pl.semaphore_signal(barrier, inc=1, device_id=partner, device_id_type=MESH)
    for piece in range(4):
        load(piece).start()
    tables_in = [
        pltpu.make_async_copy(source, target, side_sem.at[index])
        for index, (source, target) in enumerate((
            (near_hbm, near), (first_hbm, first), (second_hbm, second), (third_hbm, third),
            (spectral_hbm, spectral), (outer_hbm, outer), (coupling_hbm, coupling)))
    ]
    for copy in tables_in:
        copy.start()

    def send(flow, stage, source, target, to):
        pltpu.make_async_remote_copy(
            src_ref=source, dst_ref=target, send_sem=send_sem.at[flow, stage],
            recv_sem=recv_sem.at[flow, stage], device_id=to, device_id_type=MESH,
        ).start()

    def whole(flow, stage, rows):
        ref = part.at[0, pl.ds(0, rows)]
        return pltpu.make_async_remote_copy(
            src_ref=ref, dst_ref=ref, send_sem=send_sem.at[flow, stage],
            recv_sem=recv_sem.at[flow, stage], device_id=twin, device_id_type=MESH,
        )

    def arrived(flow, stage, rows):
        whole(flow, stage, rows).wait_recv()

    def own(flow, depth):
        field, half, order = FLOWS[flow]
        begin = half * HALF + core * 512
        for level in range(depth):
            begin = begin + place[order[level]] * PARTS[level]
        return begin

    def partial(piece):
        half, side = pieces[piece]
        begin = begin_of(piece)
        load(piece).wait()

        @pl.loop(0, 8)
        def rows_of(step):
            for sub in range(8):
                row = pl.multiple_of(begin + step * 64 + sub * 8, 8)
                a, b, c, d = (raw[pl.ds(row * 4 + k, 8, stride=4), :] for k in range(4))
                part[0, pl.ds(row, 8), :] = c * c + d * d
                part[1, pl.ds(row, 8), :] = a * c + b * d
                part[2, pl.ds(row, 8), :] = b * c - a * d

        if piece == 0:
            pl.semaphore_wait(barrier, len(partners))
        if side == 0:
            for flow, (field, flow_half, _) in enumerate(FLOWS):
                if flow_half == half:
                    rows = pl.ds(pl.multiple_of(begin, 8), 512)
                    send(flow, 0, part.at[field, rows], met.at[flow], twin)

    def add_core(flow):
        field = FLOWS[flow][0]
        begin = own(flow, 0)
        arrived(flow, 0, 512)

        @pl.loop(0, 4)
        def add(step):
            rows = pl.ds(pl.multiple_of(begin + step * 128, 8), 128)
            part[field, rows, :] = part[field, rows, :] + met[flow, pl.ds(step * 128, 128), :]

        scatter(flow)

    def scatter(flow):
        field, _, order = FLOWS[flow]
        for shift in (2, 1, 3):
            peer = (place[order[0]] + shift) % 4
            rows = pl.ds(pl.multiple_of(own(flow, 0) + peer * 128, 8), 128)
            send(flow, 1, part.at[field, rows], got1.at[flow, pl.ds((3 - shift) * 128, 128)], device(order[0], shift))

    def each_peer(flow, call):
        _, second_axis, third_axis = FLOWS[flow][2]

        @pl.loop(1, 16)
        def peers(index):
            shifts = (index // 4, index % 4)
            at = dict(place)
            at[second_axis] = (place[second_axis] + shifts[0]) % 4
            at[third_axis] = (place[third_axis] + shifts[1]) % 4
            call(shifts, at[second_axis] * 32 + at[third_axis] * 8,
                 (at["z"] % 2 * 2 + core, at["x"] * 8 + at["z"] // 2 * 4 + at["y"]))

    def add_line(flow):
        field = FLOWS[flow][0]
        begin = pl.multiple_of(own(flow, 1), 8)
        arrived(flow, 1, 384)
        rows = pl.ds(begin, 128)
        total = part[field, rows, :]
        for slot in range(3):
            total = total + got1[flow, pl.ds(slot * 128, 128), :]
        part[field, rows, :] = total

        def call(shifts, offset, to):
            slot = (4 - shifts[0]) % 4 * 4 + (4 - shifts[1]) % 4 - 1
            send(flow, 2, part.at[field, pl.ds(pl.multiple_of(begin + offset, 8), 8)],
                 got2.at[flow, pl.ds(pl.multiple_of(slot * 8, 8), 8)], to)

        each_peer(flow, call)

    def add_layer(flow):
        field = FLOWS[flow][0]
        arrived(flow, 2, 120)
        rows = pl.ds(pl.multiple_of(own(flow, 3), 8), 8)
        terms = [part[field, rows, :]] + [got2[flow, pl.ds(slot * 8, 8), :] for slot in range(15)]
        while len(terms) > 1:
            terms = [terms[k] + terms[k + 1] for k in range(0, len(terms), 2)]
        full[field, rows, :] = terms[0] * (1.0 / 128.0)
        each_peer(flow, lambda shifts, offset, to: send(flow, 3, full.at[field, rows], full.at[field, rows], to))

    def spread(flow):
        field, _, order = FLOWS[flow]
        arrived(flow, 3, 120)
        rows = pl.ds(pl.multiple_of(own(flow, 1), 8), 128)
        for shift in (2, 1, 3):
            send(flow, 4, full.at[field, rows], full.at[field, rows], device(order[0], shift))

    def share(flow):
        field = FLOWS[flow][0]
        arrived(flow, 4, 384)
        rows = pl.ds(pl.multiple_of(own(flow, 0), 8), 512)
        send(flow, 5, full.at[field, rows], full.at[field, rows], twin)

    def thrice(values):
        high, low = high_low(values)
        return jnp.concatenate([high, low, high], axis=0)

    def across_planes(source, target):
        for step in range(8):
            slices = [pl.ds(step * 4 + k, N, stride=32) for k in range(4)]
            values = jnp.concatenate([source[s, :] for s in slices], axis=1)
            values = jnp.dot(first[...], thrice(values), preferred_element_type=f32)
            values = values * jnp.concatenate([spectral[s, :] for s in slices], axis=1)
            values = jnp.dot(first[...], thrice(values), preferred_element_type=f32)
            for k in range(4):
                target[slices[k], :] = values[:, 128 * k:128 * k + 128]

    even = jnp.where(lax.broadcasted_iota(jnp.int32, (32, 1024), 1) % 128 < 64, 1.0, 0.0).astype(bf16)

    def within_planes(source, base, level=None):
        values = jnp.concatenate([source[pl.ds(base + 32 * k, 32), :] for k in range(8)], axis=1)
        if level is not None:
            values = values - level
        high, low = high_low(values)
        high0, low0 = high * even, low * even
        high1, low1 = high - high0, low - low0
        mixed = jnp.dot(second[...], jnp.concatenate([high0, high1, low0, low1, high0, high1], axis=0),
                        preferred_element_type=f32)
        high, low = high_low(jnp.concatenate([
            jnp.concatenate([mixed[0:32, 128 * k:128 * k + 128], mixed[32:64, 128 * k:128 * k + 128]], axis=1)
            for k in range(8)], axis=0))
        both = jnp.dot(high, third[...], preferred_element_type=f32)
        return both[:, 0:128] + (both[:, 128:256] + jnp.dot(low, third[:, 0:128], preferred_element_type=f32))

    def prepare():
        @pl.loop(0, 32)
        def planes(pair):
            for plane in (pair * 2, pair * 2 + 1):
                for component in range(4):
                    for block in range(4):
                        put(start, component, plane, block,
                            raw[pl.ds(plane * 128 + block * 32 + component, 8, stride=4), :])

    def opening_laplace(begin, end):
        upper = lax.broadcasted_iota(jnp.int32, (8, 128), 1) >= 64

        @pl.loop(begin, end)
        def groups(index):
            plane0 = index * GROUP
            beside_planes(start, near, beside, plane0)
            for sub in range(GROUP):
                plane = plane0 + sub
                for block in range(4):
                    rows = pl.ds(pl.multiple_of(plane * 32, 32) + 8 * block, 8)
                    for component in range(4):
                        laplace[component, rows, :] = neighbours(
                            start, beside, upper, plane, sub, component, 8 * block)[1]

    lead, rest = (0, 1), (2, 3, 4, 5)

    def each(flows, call, *levels):
        for flow in flows:
            call(flow, *levels)

    partial(0)
    partial(1)
    partial(2)
    add_core(0)
    partial(3)
    add_core(1)
    each(rest, add_core)
    prepare()
    for copy in tables_in:
        copy.wait()
    each(lead, add_line)
    opening_laplace(0, 3)
    each(rest, add_line)
    opening_laplace(3, 8)
    each(lead, add_layer)
    each(rest, add_layer)
    each(lead, spread)
    each(rest, spread)
    each(lead, share)
    mine = [pl.multiple_of(own(flow, 0) + part_row, 256) for flow in lead for part_row in (0, 256)]
    other = [pl.multiple_of(base + 512 - 1024 * core, 256) for base in mine]
    total = full[0, pl.ds(mine[0], 64), :]
    for base in mine:
        for row in range(0, 256, 64):
            if base is not mine[0] or row:
                total = total + full[0, pl.ds(base + row, 64), :]
    level = jnp.sum(total) * (1.0 / (1024 * 128))
    for base in mine:
        work[pl.ds(base, 256), :] = within_planes(full.at[0], base, level)
    each(lead, lambda flow: arrived(flow, 5, 512))
    for base in other:
        work[pl.ds(base, 256), :] = within_planes(full.at[0], base, level)
    each(rest, share)
    across_planes(work, hill)
    for step in range(8):
        rows = pl.ds(step * 256, 256)
        fields[0, rows, :] = 2.0 * (outer[rows, :] + full[0, rows, :] + within_planes(hill, step * 256)) + 6.0
    each(rest, lambda flow: arrived(flow, 5, 512))

    upper = lax.broadcasted_iota(jnp.int32, (8, 128), 1) >= 64

    def combine(plane, block, state, total, factor, store, held_fields=None):
        rows = pl.ds(pl.multiple_of(plane * 32, 32) + 8 * block, 8)
        mean, real, imag = held_fields or (fields[0, rows, :], fields[1, rows, :], fields[2, rows, :])
        a, b, c, d = state
        made = [mean * a - total[0] + (real * c - imag * d),
                mean * b - total[1] + (real * d + imag * c),
                (real * a + imag * b) - (mean * c - total[2]),
                (real * b - imag * a) - (mean * d - total[3])]
        old = [start[component, pl.ds(plane * PITCH + 8 + 8 * block, 8), :] for component in range(4)]
        half = 0.5 * factor
        store(plane, block, [old[0] + half * made[1], old[1] - half * made[0],
                             old[2] + half * made[3], old[3] - half * made[2]])

    def step(source, factor, store):
        def group(index):
            plane0 = index * GROUP
            beside_planes(source, near, beside, plane0)
            for sub in range(GROUP):
                for block in range(4):
                    both = [neighbours(source, beside, upper, plane0 + sub, sub, component, 8 * block)
                            for component in range(4)]
                    combine(plane0 + sub, block, [b[0] for b in both], [b[1] for b in both], factor, store)
        return group

    def into(state):
        def store(plane, block, values):
            for component in range(4):
                put(state, component, plane, block, values[component])
        return store

    def finish(plane, block, values):
        for component in range(4):
            raw[pl.ds(plane * 128 + block * 32 + component, 8, stride=4), :] = values[component]

    @pl.loop(0, N // 4)
    def opening(index):
        for sub in range(4):
            plane = index * 4 + sub
            for block in range(4):
                rows = pl.ds(pl.multiple_of(plane * 32, 32) + 8 * block, 8)
                scale = -2.0 * coupling[rows, :]
                real, imag = scale * full[1, rows, :], scale * full[2, rows, :]
                fields[1, rows, :] = real
                fields[2, rows, :] = imag
                state = [start[component, pl.ds(plane * PITCH + 8 + 8 * block, 8), :] for component in range(4)]
                total = [laplace[component, rows, :] for component in range(4)]
                combine(plane, block, state, total, time_step / 4, into(ping), (fields[0, rows, :], real, imag))

    held = pl.ds(lax.axis_index("grp") * 512 + lax.axis_index("wf"), 16, stride=32)
    potentials[0] = 0.5 * fields[0, held, :] - 3.0
    potentials[1] = 0.5 * fields[1, held, :]
    potentials[2] = 0.5 * fields[2, held, :]
    for source, degree, target in ((ping, 3, pong), (pong, 2, ping)):
        pl.loop(0, N // GROUP)(step(source, time_step / degree, into(target)))
    last = step(ping, time_step, finish)

    def save(index):
        rows = pl.ds(index * 1024, 1024)
        return pltpu.make_async_copy(raw.at[rows], out_hbm.at[rows], out_sem.at[index])

    @pl.loop(0, N // GROUP)
    def closing(index):
        last(index)
        save(index).start()

    for index in range(N // GROUP):
        save(index).wait()
    for flow in lead + rest:
        for stage, rows in enumerate((512, 384, 120, 120, 384, 512)):
            whole(flow, stage, rows).wait_send()


def copy_kernel(evolved_in, potentials_in, evolved, potentials, lines, small, in_sem, out_sem):
    pairs = [(evolved_in.at[rows], lines.at[rows], evolved.at[rows])
             for rows in (pl.ds(index * 1024, 1024) for index in range(8))]
    pairs.append((potentials_in, small, potentials))
    arrive = [pltpu.make_async_copy(a, b, in_sem.at[index]) for index, (a, b, _) in enumerate(pairs)]
    leave = [pltpu.make_async_copy(b, c, out_sem.at[index]) for index, (_, b, c) in enumerate(pairs)]
    for copy in arrive:
        copy.start()
    for come, go in zip(arrive, leave):
        come.wait()
        go.start()
    for copy in leave:
        copy.wait()


def local(quasi, outer_field, coupling):
    rows = quasi.reshape(4, ROWS, 128).transpose(1, 0, 2).reshape(4 * ROWS, 128)
    far = pl.BlockSpec(memory_space=pltpu.HBM)
    inside = pl.BlockSpec(memory_space=pltpu.VMEM)
    weights = [jnp.asarray(w) for w in tables()]
    shape = jax.ShapeDtypeStruct
    state = pltpu.VMEM((4, PADDED, 128), f32)
    field = pltpu.VMEM((ROWS, 128), f32)
    evolved, potentials = pl.pallas_call(
        kernel,
        out_shape=(shape((4 * ROWS, 128), f32), shape((3, 16, 128), f32)),
        in_specs=[far] * 8,
        out_specs=(far, inside),
        scratch_shapes=[
            pltpu.VMEM((4 * ROWS, 128), f32),
            pltpu.VMEM((3, ROWS, 128), f32),
            state,
            pltpu.VMEM((4, ROWS, 128), f32),
            state,
            state,
            pltpu.VMEM((3, ROWS, 128), f32),
            pltpu.VMEM((3, ROWS, 128), f32),
            pltpu.VMEM((6, 512, 128), f32),
            pltpu.VMEM((6, 384, 128), f32),
            pltpu.VMEM((6, 120, 128), f32),
            field,
            field,
        ] + [pltpu.VMEM(w.shape, w.dtype) for w in weights] + [
            field,
            field,
            pltpu.VMEM((GROUP * 128, 128), f32),
            pltpu.SemaphoreType.DMA((4,)),
            pltpu.SemaphoreType.DMA((6, 6)),
            pltpu.SemaphoreType.DMA((6, 6)),
            pltpu.SemaphoreType.DMA((7,)),
            pltpu.SemaphoreType.DMA((N // GROUP,)),
        ],
        compiler_params=pltpu.CompilerParams(
            collective_id=0, has_side_effects=True, vmem_limit_bytes=VMEM_MIB * 2**20),
        name="superfluid",
    )(rows, outer_field.reshape(ROWS, 128), coupling.reshape(ROWS, 128), *weights)
    evolved, potentials = pl.pallas_call(
        copy_kernel,
        out_shape=(shape((4 * ROWS, 128), f32), shape((3, 16, 128), f32)),
        in_specs=[far] * 2,
        out_specs=(far,) * 2,
        scratch_shapes=[
            pltpu.VMEM((4 * ROWS, 128), f32),
            pltpu.VMEM((3, 16, 128), f32),
            pltpu.SemaphoreType.DMA((9,)),
            pltpu.SemaphoreType.DMA((9,)),
        ],
        compiler_params=pltpu.CompilerParams(vmem_limit_bytes=VMEM_MIB * 2**20),
        name="deliver",
    )(evolved, potentials)
    evolved = evolved.reshape(ROWS, 4, 128).transpose(1, 0, 2).reshape(1, 4, ROWS * 128)
    return evolved, potentials


def solution(mesh):
    return jax.shard_map(
        local,
        mesh=mesh,
        in_specs=(P(("grp", "wf"), None, None), P(), P()),
        out_specs=(P(("grp", "wf"), None, None), P(None, "grp", "wf")),
        check_vma=False,
    )
```

```python
import math

import jax
import jax.numpy as jnp
import numpy as np
from jax import lax
from jax.experimental import pallas as pl
from jax.experimental.pallas import tpu as pltpu
from jax.sharding import PartitionSpec as P

MESH = pl.DeviceIdType.MESH
N = 64
ROWS = 2048
HALF = 1024
PITCH = 40
PADDED = N * PITCH + 8
GROUP = 16
VMEM_MIB = 58
time_step = 0.2
f32 = jnp.float32
bf16 = jnp.bfloat16

FLOWS = [(0, 0, "xyz"), (0, 1, "yzx"), (1, 0, "zxy"), (1, 1, "xyz"), (2, 0, "yzx"), (2, 1, "zxy")]
PARTS = (128, 32, 8)


def high_low(values):
    high = values.astype(bf16)
    return high, (values - high.astype(f32)).astype(bf16)


def tables():
    index = np.arange(N)
    angle = 2 * math.pi / N * (index[:, None] * index[None, :] % N)
    hartley = (np.cos(angle) + np.sin(angle)) / math.sqrt(N)
    symbol = 2 - 2 * np.cos(2 * math.pi / N * index)
    squared = symbol[:, None, None] + symbol[None, :, None] + symbol[None, None, :]
    spectral = np.where(squared > 0.001, 4 * math.pi * 0.25 / np.maximum(squared, 0.001), 0.0)
    spectral = spectral.reshape(ROWS, 128).astype(np.float32)

    def cut(matrix):
        high = matrix.astype(np.float32).astype(jnp.bfloat16)
        return high, (matrix - high.astype(np.float64)).astype(np.float32).astype(jnp.bfloat16)

    high, low = cut(hartley)
    first = np.concatenate([high, high, low], axis=1)
    high, low = cut(np.concatenate([
        np.concatenate([hartley[q::2, p::2] for p in range(2)], axis=1) for q in range(2)], axis=0))
    second = np.concatenate([high, high, low], axis=1)
    third = np.concatenate(cut(np.kron(np.eye(2), np.concatenate([hartley, hartley], axis=0))), axis=1)
    lane = np.arange(128)
    near = np.zeros((128, 128), np.float32)
    near[(lane & 64) | ((lane + 1) & 63), lane] += 1
    near[(lane & 64) | ((lane + 63) & 63), lane] += 1
    near = np.concatenate([near, near], axis=0).astype(jnp.bfloat16)
    return first, second, third, spectral, near


def put(state, component, plane, block, values):
    base = plane * PITCH + 8
    state[component, pl.ds(base + 8 * block, 8), :] = values
    if block == 0:
        state[component, pl.ds(base + 32, 1), :] = values[0:1]
    if block == 3:
        state[component, pl.ds(base - 1, 1), :] = values[7:8]


def beside_planes(source, near, beside, plane0):
    lines = []
    for sub in range(GROUP):
        for component in range(4):
            values = source[component, pl.ds((plane0 + sub) * PITCH + 8, 32), :]
            lines.append(jnp.concatenate(high_low(values), axis=1))
    beside[...] = jnp.dot(jnp.concatenate(lines, axis=0), near[...], preferred_element_type=f32)


def neighbours(source, beside, upper, plane, sub, component, row):
    base = plane * PITCH + 8
    before = lax.rem(plane + N - 1, N) * PITCH + 8
    after = lax.rem(plane + 1, N) * PITCH + 8
    here = source[component, pl.ds(base + row, 8), :]
    up = source[component, pl.ds(base + row - 1, 8), :]
    down = source[component, pl.ds(base + row + 1, 8), :]
    across = pltpu.roll(here + jnp.where(upper, up, down), 64, 1)
    along = source[component, pl.ds(before + row, 8), :] + source[component, pl.ds(after + row, 8), :]
    return here, beside[pl.ds((sub * 4 + component) * 32 + row, 8), :] + along + across


def kernel(q_hbm, outer_hbm, coupling_hbm, first_hbm, second_hbm, third_hbm, spectral_hbm, near_hbm,
           out_hbm, potentials, raw, fields, start, laplace, ping, pong, part, full, met, got1, got2,
           outer, coupling, first, second, third, spectral, near, work, hill, beside,
           in_sem, send_sem, recv_sem, side_sem, out_sem):
    grp, wf = lax.axis_index("grp"), lax.axis_index("wf")
    core = grp % 2
    place = {"x": wf // 8, "y": wf % 4, "z": (wf // 4 % 2) * 2 + grp // 2}

    def device(axis, shift):
        at = dict(place)
        at[axis] = (place[axis] + shift) % 4
        return (at["z"] % 2 * 2 + core, at["x"] * 8 + at["z"] // 2 * 4 + at["y"])

    twin = (grp // 2 * 2 + 1 - core, wf)
    pieces = ((0, 0), (1, 0), (0, 1), (1, 1))

    def begin_of(piece):
        half, side = pieces[piece]
        return half * HALF + jnp.where(core == side, 512, 0)

    def load(piece):
        rows = pl.ds(pl.multiple_of(begin_of(piece) * 4, 8), 2048)
        return pltpu.make_async_copy(q_hbm.at[rows], raw.at[rows], in_sem.at[piece])

    barrier = pltpu.get_barrier_semaphore()
    partners = [device(axis, shift) for axis in "xyz" for shift in (2, 1, 3)] + [twin]
    for partner in partners:
        pl.semaphore_signal(barrier, inc=1, device_id=partner, device_id_type=MESH)
    for piece in range(4):
        load(piece).start()
    tables_in = [
        pltpu.make_async_copy(source, target, side_sem.at[index])
        for index, (source, target) in enumerate((
            (near_hbm, near), (first_hbm, first), (second_hbm, second), (third_hbm, third),
            (spectral_hbm, spectral), (outer_hbm, outer), (coupling_hbm, coupling)))
    ]
    for copy in tables_in:
        copy.start()

    def send(flow, stage, source, target, to):
        pltpu.make_async_remote_copy(
            src_ref=source, dst_ref=target, send_sem=send_sem.at[flow, stage],
            recv_sem=recv_sem.at[flow, stage], device_id=to, device_id_type=MESH,
        ).start()

    def whole(flow, stage, rows):
        ref = part.at[0, pl.ds(0, rows)]
        return pltpu.make_async_remote_copy(
            src_ref=ref, dst_ref=ref, send_sem=send_sem.at[flow, stage],
            recv_sem=recv_sem.at[flow, stage], device_id=twin, device_id_type=MESH,
        )

    def arrived(flow, stage, rows):
        whole(flow, stage, rows).wait_recv()

    def own(flow, depth):
        field, half, order = FLOWS[flow]
        begin = half * HALF + core * 512
        for level in range(depth):
            begin = begin + place[order[level]] * PARTS[level]
        return begin

    def partial(piece):
        half, side = pieces[piece]
        begin = begin_of(piece)
        load(piece).wait()

        @pl.loop(0, 8)
        def rows_of(step):
            for sub in range(8):
                row = pl.multiple_of(begin + step * 64 + sub * 8, 8)
                a, b, c, d = (raw[pl.ds(row * 4 + k, 8, stride=4), :] for k in range(4))
                part[0, pl.ds(row, 8), :] = c * c + d * d
                part[1, pl.ds(row, 8), :] = a * c + b * d
                part[2, pl.ds(row, 8), :] = b * c - a * d

        if piece == 0:
            pl.semaphore_wait(barrier, len(partners))
        if side == 0:
            for flow, (field, flow_half, _) in enumerate(FLOWS):
                if flow_half == half:
                    rows = pl.ds(pl.multiple_of(begin, 8), 512)
                    send(flow, 0, part.at[field, rows], met.at[flow], twin)

    def add_core(flow):
        field = FLOWS[flow][0]
        begin = own(flow, 0)
        arrived(flow, 0, 512)

        @pl.loop(0, 4)
        def add(step):
            rows = pl.ds(pl.multiple_of(begin + step * 128, 8), 128)
            part[field, rows, :] = part[field, rows, :] + met[flow, pl.ds(step * 128, 128), :]

        scatter(flow)

    def scatter(flow):
        field, _, order = FLOWS[flow]
        for shift in (2, 1, 3):
            peer = (place[order[0]] + shift) % 4
            rows = pl.ds(pl.multiple_of(own(flow, 0) + peer * 128, 8), 128)
            send(flow, 1, part.at[field, rows], got1.at[flow, pl.ds((3 - shift) * 128, 128)], device(order[0], shift))

    def each_peer(flow, call):
        _, second_axis, third_axis = FLOWS[flow][2]

        @pl.loop(1, 16)
        def peers(index):
            shifts = (index // 4, index % 4)
            at = dict(place)
            at[second_axis] = (place[second_axis] + shifts[0]) % 4
            at[third_axis] = (place[third_axis] + shifts[1]) % 4
            call(shifts, at[second_axis] * 32 + at[third_axis] * 8,
                 (at["z"] % 2 * 2 + core, at["x"] * 8 + at["z"] // 2 * 4 + at["y"]))

    def add_line(flow):
        field = FLOWS[flow][0]
        begin = pl.multiple_of(own(flow, 1), 8)
        rows = pl.ds(begin, 128)
        total = part[field, rows, :]
        for slot in range(3):
            total = total + got1[flow, pl.ds(slot * 128, 128), :]
        part[field, rows, :] = total

        def call(shifts, offset, to):
            slot = (4 - shifts[0]) % 4 * 4 + (4 - shifts[1]) % 4 - 1
            send(flow, 2, part.at[field, pl.ds(pl.multiple_of(begin + offset, 8), 8)],
                 got2.at[flow, pl.ds(pl.multiple_of(slot * 8, 8), 8)], to)

        each_peer(flow, call)

    def add_layer(flow):
        field = FLOWS[flow][0]
        arrived(flow, 2, 120)
        rows = pl.ds(pl.multiple_of(own(flow, 3), 8), 8)
        terms = [part[field, rows, :]] + [got2[flow, pl.ds(slot * 8, 8), :] for slot in range(15)]
        while len(terms) > 1:
            terms = [terms[k] + terms[k + 1] for k in range(0, len(terms), 2)]
        full[field, rows, :] = terms[0] * (1.0 / 128.0)
        each_peer(flow, lambda shifts, offset, to: send(flow, 3, full.at[field, rows], full.at[field, rows], to))

    def spread(flow):
        field, _, order = FLOWS[flow]
        arrived(flow, 3, 120)
        rows = pl.ds(pl.multiple_of(own(flow, 1), 8), 128)
        for shift in (2, 1, 3):
            send(flow, 4, full.at[field, rows], full.at[field, rows], device(order[0], shift))

    def share(flow):
        field = FLOWS[flow][0]
        arrived(flow, 4, 384)
        rows = pl.ds(pl.multiple_of(own(flow, 0), 8), 512)
        send(flow, 5, full.at[field, rows], full.at[field, rows], twin)

    def thrice(values):
        high, low = high_low(values)
        return jnp.concatenate([high, low, high], axis=0)

    def across_planes(source, target):
        for step in range(8):
            slices = [pl.ds(step * 4 + k, N, stride=32) for k in range(4)]
            values = jnp.concatenate([source[s, :] for s in slices], axis=1)
            values = jnp.dot(first[...], thrice(values), preferred_element_type=f32)
            values = values * jnp.concatenate([spectral[s, :] for s in slices], axis=1)
            values = jnp.dot(first[...], thrice(values), preferred_element_type=f32)
            for k in range(4):
                target[slices[k], :] = values[:, 128 * k:128 * k + 128]

    even = jnp.where(lax.broadcasted_iota(jnp.int32, (32, 1024), 1) % 128 < 64, 1.0, 0.0).astype(bf16)

    def within_planes(source, base, level=None):
        values = jnp.concatenate([source[pl.ds(base + 32 * k, 32), :] for k in range(8)], axis=1)
        if level is not None:
            values = values - level
        high, low = high_low(values)
        high0, low0 = high * even, low * even
        high1, low1 = high - high0, low - low0
        mixed = jnp.dot(second[...], jnp.concatenate([high0, high1, low0, low1, high0, high1], axis=0),
                        preferred_element_type=f32)
        high, low = high_low(jnp.concatenate([
            jnp.concatenate([mixed[0:32, 128 * k:128 * k + 128], mixed[32:64, 128 * k:128 * k + 128]], axis=1)
            for k in range(8)], axis=0))
        both = jnp.dot(high, third[...], preferred_element_type=f32)
        return both[:, 0:128] + (both[:, 128:256] + jnp.dot(low, third[:, 0:128], preferred_element_type=f32))

    def prepare():
        @pl.loop(0, 32)
        def planes(pair):
            for plane in (pair * 2, pair * 2 + 1):
                for component in range(4):
                    for block in range(4):
                        put(start, component, plane, block,
                            raw[pl.ds(plane * 128 + block * 32 + component, 8, stride=4), :])

    def opening_laplace(begin, end):
        upper = lax.broadcasted_iota(jnp.int32, (8, 128), 1) >= 64

        @pl.loop(begin, end)
        def groups(index):
            plane0 = index * GROUP
            beside_planes(start, near, beside, plane0)
            for sub in range(GROUP):
                plane = plane0 + sub
                for block in range(4):
                    rows = pl.ds(pl.multiple_of(plane * 32, 32) + 8 * block, 8)
                    for component in range(4):
                        laplace[component, rows, :] = neighbours(
                            start, beside, upper, plane, sub, component, 8 * block)[1]

    lead, rest = (0, 1), (2, 4, 3, 5)

    def each(flows, call, *levels):
        for flow in flows:
            call(flow, *levels)

    partial(0)
    partial(1)
    partial(2)
    add_core(0)
    partial(3)
    add_core(1)
    each(rest, add_core)
    prepare()
    for copy in tables_in:
        copy.wait()
    each(lead, lambda flow: arrived(flow, 1, 384))
    each(lead, add_line)
    opening_laplace(0, 2)
    for flow in rest:
        arrived(flow, 1, 384)
        add_line(flow)
    opening_laplace(2, 4)
    each(lead, add_layer)
    each(rest, add_layer)
    each(lead, spread)
    each(rest, spread)
    each(lead, share)
    mine = [pl.multiple_of(own(flow, 0) + part_row, 256) for flow in lead for part_row in (0, 256)]
    other = [pl.multiple_of(base + 512 - 1024 * core, 256) for base in mine]
    total = full[0, pl.ds(mine[0], 64), :]
    for base in mine:
        for row in range(0, 256, 64):
            if base is not mine[0] or row:
                total = total + full[0, pl.ds(base + row, 64), :]
    level = jnp.sum(total) * (1.0 / (1024 * 128))
    for base in mine:
        work[pl.ds(base, 256), :] = within_planes(full.at[0], base, level)
    each(lead, lambda flow: arrived(flow, 5, 512))
    for base in other:
        work[pl.ds(base, 256), :] = within_planes(full.at[0], base, level)
    each(rest, share)
    across_planes(work, hill)
    for step in range(8):
        rows = pl.ds(step * 256, 256)
        fields[0, rows, :] = 2.0 * (outer[rows, :] + full[0, rows, :] + within_planes(hill, step * 256)) + 6.0
    upper = lax.broadcasted_iota(jnp.int32, (8, 128), 1) >= 64

    def combine(plane, block, state, total, factor, store, held_fields=None):
        rows = pl.ds(pl.multiple_of(plane * 32, 32) + 8 * block, 8)
        mean, real, imag = held_fields or (fields[0, rows, :], fields[1, rows, :], fields[2, rows, :])
        a, b, c, d = state
        made = [mean * a - total[0] + (real * c - imag * d),
                mean * b - total[1] + (real * d + imag * c),
                (real * a + imag * b) - (mean * c - total[2]),
                (real * b - imag * a) - (mean * d - total[3])]
        old = [start[component, pl.ds(plane * PITCH + 8 + 8 * block, 8), :] for component in range(4)]
        half = 0.5 * factor
        store(plane, block, [old[0] + half * made[1], old[1] - half * made[0],
                             old[2] + half * made[3], old[3] - half * made[2]])

    def step(source, factor, store):
        def group(index):
            plane0 = index * GROUP
            beside_planes(source, near, beside, plane0)
            for sub in range(GROUP):
                for block in range(4):
                    both = [neighbours(source, beside, upper, plane0 + sub, sub, component, 8 * block)
                            for component in range(4)]
                    combine(plane0 + sub, block, [b[0] for b in both], [b[1] for b in both], factor, store)
        return group

    def into(state):
        def store(plane, block, values):
            for component in range(4):
                put(state, component, plane, block, values[component])
        return store

    def finish(plane, block, values):
        for component in range(4):
            raw[pl.ds(plane * 128 + block * 32 + component, 8, stride=4), :] = values[component]

    def opening(index):
        for sub in range(4):
            plane = index * 4 + sub
            for block in range(4):
                rows = pl.ds(pl.multiple_of(plane * 32, 32) + 8 * block, 8)
                scale = -2.0 * coupling[rows, :]
                real, imag = scale * full[1, rows, :], scale * full[2, rows, :]
                fields[1, rows, :] = real
                fields[2, rows, :] = imag
                state = [start[component, pl.ds(plane * PITCH + 8 + 8 * block, 8), :] for component in range(4)]
                total = [laplace[component, rows, :] for component in range(4)]
                combine(plane, block, state, total, time_step / 4, into(ping), (fields[0, rows, :], real, imag))

    for half in range(2):
        each(rest[2 * half:2 * half + 2], lambda flow: arrived(flow, 5, 512))
        pl.loop(half * 8, half * 8 + 8)(opening)
    held = pl.ds(lax.axis_index("grp") * 512 + lax.axis_index("wf"), 16, stride=32)
    potentials[0] = 0.5 * fields[0, held, :] - 3.0
    potentials[1] = 0.5 * fields[1, held, :]
    potentials[2] = 0.5 * fields[2, held, :]
    for source, degree, target in ((ping, 3, pong), (pong, 2, ping)):
        pl.loop(0, N // GROUP)(step(source, time_step / degree, into(target)))
    last = step(ping, time_step, finish)

    def save(index):
        rows = pl.ds(index * 2048, 2048)
        return pltpu.make_async_copy(raw.at[rows], out_hbm.at[rows], out_sem.at[index])

    @pl.loop(0, N // GROUP)
    def closing(index):
        last(index)
        save(index).start()

    for index in range(N // GROUP):
        save(index).wait()
    for flow in lead + rest:
        for stage, rows in enumerate((512, 384, 120, 120, 384, 512)):
            whole(flow, stage, rows).wait_send()


def copy_kernel(evolved_in, potentials_in, evolved, potentials, lines, small, in_sem, out_sem):
    pairs = [(evolved_in.at[rows], lines.at[rows], evolved.at[rows])
             for rows in (pl.ds(index * 1024, 1024) for index in range(8))]
    pairs.append((potentials_in, small, potentials))
    arrive = [pltpu.make_async_copy(a, b, in_sem.at[index]) for index, (a, b, _) in enumerate(pairs)]
    leave = [pltpu.make_async_copy(b, c, out_sem.at[index]) for index, (_, b, c) in enumerate(pairs)]
    for copy in arrive:
        copy.start()
    for come, go in zip(arrive, leave):
        come.wait()
        go.start()
    for copy in leave:
        copy.wait()


def local(quasi, outer_field, coupling):
    rows = quasi.reshape(4, ROWS, 128).transpose(1, 0, 2).reshape(4 * ROWS, 128)
    far = pl.BlockSpec(memory_space=pltpu.HBM)
    inside = pl.BlockSpec(memory_space=pltpu.VMEM)
    weights = [jnp.asarray(w) for w in tables()]
    shape = jax.ShapeDtypeStruct
    state = pltpu.VMEM((4, PADDED, 128), f32)
    field = pltpu.VMEM((ROWS, 128), f32)
    evolved, potentials = pl.pallas_call(
        kernel,
        out_shape=(shape((4 * ROWS, 128), f32), shape((3, 16, 128), f32)),
        in_specs=[far] * 8,
        out_specs=(far, inside),
        scratch_shapes=[
            pltpu.VMEM((4 * ROWS, 128), f32),
            pltpu.VMEM((3, ROWS, 128), f32),
            state,
            pltpu.VMEM((4, ROWS, 128), f32),
            state,
            state,
            pltpu.VMEM((3, ROWS, 128), f32),
            pltpu.VMEM((3, ROWS, 128), f32),
            pltpu.VMEM((6, 512, 128), f32),
            pltpu.VMEM((6, 384, 128), f32),
            pltpu.VMEM((6, 120, 128), f32),
            field,
            field,
        ] + [pltpu.VMEM(w.shape, w.dtype) for w in weights] + [
            field,
            field,
            pltpu.VMEM((GROUP * 128, 128), f32),
            pltpu.SemaphoreType.DMA((4,)),
            pltpu.SemaphoreType.DMA((6, 6)),
            pltpu.SemaphoreType.DMA((6, 6)),
            pltpu.SemaphoreType.DMA((7,)),
            pltpu.SemaphoreType.DMA((N // GROUP,)),
        ],
        compiler_params=pltpu.CompilerParams(
            collective_id=0, has_side_effects=True, vmem_limit_bytes=VMEM_MIB * 2**20),
        name="superfluid",
    )(rows, outer_field.reshape(ROWS, 128), coupling.reshape(ROWS, 128), *weights)
    evolved, potentials = pl.pallas_call(
        copy_kernel,
        out_shape=(shape((4 * ROWS, 128), f32), shape((3, 16, 128), f32)),
        in_specs=[far] * 2,
        out_specs=(far,) * 2,
        scratch_shapes=[
            pltpu.VMEM((4 * ROWS, 128), f32),
            pltpu.VMEM((3, 16, 128), f32),
            pltpu.SemaphoreType.DMA((9,)),
            pltpu.SemaphoreType.DMA((9,)),
        ],
        compiler_params=pltpu.CompilerParams(vmem_limit_bytes=VMEM_MIB * 2**20),
        name="deliver",
    )(evolved, potentials)
    evolved = evolved.reshape(ROWS, 4, 128).transpose(1, 0, 2).reshape(1, 4, ROWS * 128)
    return evolved, potentials


def solution(mesh):
    return jax.shard_map(
        local,
        mesh=mesh,
        in_specs=(P(("grp", "wf"), None, None), P(), P()),
        out_specs=(P(("grp", "wf"), None, None), P(None, "grp", "wf")),
        check_vma=False,
    )
```

```python
import math

import jax
import jax.numpy as jnp
import numpy as np
from jax import lax
from jax.experimental import pallas as pl
from jax.experimental.pallas import tpu as pltpu
from jax.sharding import PartitionSpec as P

MESH = pl.DeviceIdType.MESH
N = 64
ROWS = 2048
HALF = 1024
PITCH = 40
PADDED = N * PITCH + 8
GROUP = 16
VMEM_MIB = 58
time_step = 0.2
f32 = jnp.float32
bf16 = jnp.bfloat16

FLOWS = [(0, 0, "xyz"), (0, 1, "yzx"), (1, 0, "zxy"), (1, 1, "xyz"), (2, 0, "yzx"), (2, 1, "zxy")]
PARTS = (128, 32, 8)


def high_low(values):
    high = values.astype(bf16)
    return high, (values - high.astype(f32)).astype(bf16)


def tables():
    index = np.arange(N)
    angle = 2 * math.pi / N * (index[:, None] * index[None, :] % N)
    hartley = (np.cos(angle) + np.sin(angle)) / math.sqrt(N)
    symbol = 2 - 2 * np.cos(2 * math.pi / N * index)
    squared = symbol[:, None, None] + symbol[None, :, None] + symbol[None, None, :]
    spectral = np.where(squared > 0.001, 4 * math.pi * 0.25 / np.maximum(squared, 0.001), 0.0)
    spectral = spectral.reshape(ROWS, 128).astype(np.float32)

    def cut(matrix):
        high = matrix.astype(np.float32).astype(jnp.bfloat16)
        return high, (matrix - high.astype(np.float64)).astype(np.float32).astype(jnp.bfloat16)

    high, low = cut(hartley)
    first = np.concatenate([high, high, low], axis=1)
    high, low = cut(np.concatenate([
        np.concatenate([hartley[q::2, p::2] for p in range(2)], axis=1) for q in range(2)], axis=0))
    second = np.concatenate([high, high, low], axis=1)
    third = np.concatenate(cut(np.kron(np.eye(2), np.concatenate([hartley, hartley], axis=0))), axis=1)
    lane = np.arange(128)
    near = np.zeros((128, 128), np.float32)
    near[(lane & 64) | ((lane + 1) & 63), lane] += 1
    near[(lane & 64) | ((lane + 63) & 63), lane] += 1
    near = np.concatenate([near, near], axis=0).astype(jnp.bfloat16)
    return first, second, third, spectral, near


def put(state, component, plane, block, values):
    base = plane * PITCH + 8
    state[component, pl.ds(base + 8 * block, 8), :] = values
    if block == 0:
        state[component, pl.ds(base + 32, 1), :] = values[0:1]
    if block == 3:
        state[component, pl.ds(base - 1, 1), :] = values[7:8]


def beside_planes(source, near, beside, plane0):
    lines = []
    for sub in range(GROUP):
        for component in range(4):
            values = source[component, pl.ds((plane0 + sub) * PITCH + 8, 32), :]
            lines.append(jnp.concatenate(high_low(values), axis=1))
    beside[...] = jnp.dot(jnp.concatenate(lines, axis=0), near[...], preferred_element_type=f32)


def neighbours(source, beside, upper, plane, sub, component, row):
    base = plane * PITCH + 8
    before = lax.rem(plane + N - 1, N) * PITCH + 8
    after = lax.rem(plane + 1, N) * PITCH + 8
    here = source[component, pl.ds(base + row, 8), :]
    up = source[component, pl.ds(base + row - 1, 8), :]
    down = source[component, pl.ds(base + row + 1, 8), :]
    across = pltpu.roll(here + jnp.where(upper, up, down), 64, 1)
    along = source[component, pl.ds(before + row, 8), :] + source[component, pl.ds(after + row, 8), :]
    return here, beside[pl.ds((sub * 4 + component) * 32 + row, 8), :] + along + across


def kernel(q_hbm, outer_hbm, coupling_hbm, first_hbm, second_hbm, third_hbm, spectral_hbm, near_hbm,
           out_hbm, potentials, raw, fields, start, laplace, ping, pong, part, full, met, got1, got2,
           outer, coupling, first, second, third, spectral, near, work, hill, beside,
           in_sem, send_sem, recv_sem, side_sem, out_sem):
    grp, wf = lax.axis_index("grp"), lax.axis_index("wf")
    core = grp % 2
    place = {"x": wf // 8, "y": wf % 4, "z": (wf // 4 % 2) * 2 + grp // 2}

    def device(axis, shift):
        at = dict(place)
        at[axis] = (place[axis] + shift) % 4
        return (at["z"] % 2 * 2 + core, at["x"] * 8 + at["z"] // 2 * 4 + at["y"])

    twin = (grp // 2 * 2 + 1 - core, wf)
    pieces = ((0, 0), (1, 0), (0, 1), (1, 1))

    def begin_of(piece):
        half, side = pieces[piece]
        return half * HALF + jnp.where(core == side, 512, 0)

    def load(piece):
        rows = pl.ds(pl.multiple_of(begin_of(piece) * 4, 8), 2048)
        return pltpu.make_async_copy(q_hbm.at[rows], raw.at[rows], in_sem.at[piece])

    barrier = pltpu.get_barrier_semaphore()
    partners = [device(axis, shift) for axis in "xyz" for shift in (2, 1, 3)] + [twin]
    for partner in partners:
        pl.semaphore_signal(barrier, inc=1, device_id=partner, device_id_type=MESH)
    for piece in range(4):
        load(piece).start()
    tables_in = [
        pltpu.make_async_copy(source, target, side_sem.at[index])
        for index, (source, target) in enumerate((
            (near_hbm, near), (first_hbm, first), (second_hbm, second), (third_hbm, third),
            (spectral_hbm, spectral), (outer_hbm, outer), (coupling_hbm, coupling)))
    ]
    for copy in tables_in:
        copy.start()

    def send(flow, stage, source, target, to):
        pltpu.make_async_remote_copy(
            src_ref=source, dst_ref=target, send_sem=send_sem.at[flow, stage],
            recv_sem=recv_sem.at[flow, stage], device_id=to, device_id_type=MESH,
        ).start()

    def whole(flow, stage, rows):
        ref = part.at[0, pl.ds(0, rows)]
        return pltpu.make_async_remote_copy(
            src_ref=ref, dst_ref=ref, send_sem=send_sem.at[flow, stage],
            recv_sem=recv_sem.at[flow, stage], device_id=twin, device_id_type=MESH,
        )

    def arrived(flow, stage, rows):
        whole(flow, stage, rows).wait_recv()

    def own(flow, depth):
        field, half, order = FLOWS[flow]
        begin = half * HALF + core * 512
        for level in range(depth):
            begin = begin + place[order[level]] * PARTS[level]
        return begin

    def partial(piece):
        half, side = pieces[piece]
        begin = begin_of(piece)
        load(piece).wait()

        @pl.loop(0, 8)
        def rows_of(step):
            for sub in range(8):
                row = pl.multiple_of(begin + step * 64 + sub * 8, 8)
                a, b, c, d = (raw[pl.ds(row * 4 + k, 8, stride=4), :] for k in range(4))
                part[0, pl.ds(row, 8), :] = c * c + d * d
                part[1, pl.ds(row, 8), :] = a * c + b * d
                part[2, pl.ds(row, 8), :] = b * c - a * d

        if piece == 0:
            pl.semaphore_wait(barrier, len(partners))
        if side == 0:
            for flow, (field, flow_half, _) in enumerate(FLOWS):
                if flow_half == half:
                    rows = pl.ds(pl.multiple_of(begin, 8), 512)
                    send(flow, 0, part.at[field, rows], met.at[flow], twin)

    def add_core(flow):
        field = FLOWS[flow][0]
        begin = own(flow, 0)
        arrived(flow, 0, 512)

        @pl.loop(0, 4)
        def add(step):
            rows = pl.ds(pl.multiple_of(begin + step * 128, 8), 128)
            part[field, rows, :] = part[field, rows, :] + met[flow, pl.ds(step * 128, 128), :]

        scatter(flow)

    def scatter(flow):
        field, _, order = FLOWS[flow]
        for shift in (2, 1, 3):
            peer = (place[order[0]] + shift) % 4
            rows = pl.ds(pl.multiple_of(own(flow, 0) + peer * 128, 8), 128)
            send(flow, 1, part.at[field, rows], got1.at[flow, pl.ds((3 - shift) * 128, 128)], device(order[0], shift))

    def each_peer(flow, call):
        _, second_axis, third_axis = FLOWS[flow][2]

        @pl.loop(1, 16)
        def peers(index):
            shifts = (index // 4, index % 4)
            at = dict(place)
            at[second_axis] = (place[second_axis] + shifts[0]) % 4
            at[third_axis] = (place[third_axis] + shifts[1]) % 4
            call(shifts, at[second_axis] * 32 + at[third_axis] * 8,
                 (at["z"] % 2 * 2 + core, at["x"] * 8 + at["z"] // 2 * 4 + at["y"]))

    def add_line(flow):
        field = FLOWS[flow][0]
        begin = pl.multiple_of(own(flow, 1), 8)
        rows = pl.ds(begin, 128)
        total = part[field, rows, :]
        for slot in range(3):
            total = total + got1[flow, pl.ds(slot * 128, 128), :]
        part[field, rows, :] = total

        def call(shifts, offset, to):
            slot = (4 - shifts[0]) % 4 * 4 + (4 - shifts[1]) % 4 - 1
            send(flow, 2, part.at[field, pl.ds(pl.multiple_of(begin + offset, 8), 8)],
                 got2.at[flow, pl.ds(pl.multiple_of(slot * 8, 8), 8)], to)

        each_peer(flow, call)

    def add_layer(flow):
        field = FLOWS[flow][0]
        arrived(flow, 2, 120)
        rows = pl.ds(pl.multiple_of(own(flow, 3), 8), 8)
        terms = [part[field, rows, :]] + [got2[flow, pl.ds(slot * 8, 8), :] for slot in range(15)]
        while len(terms) > 1:
            terms = [terms[k] + terms[k + 1] for k in range(0, len(terms), 2)]
        full[field, rows, :] = terms[0] * (1.0 / 128.0)
        each_peer(flow, lambda shifts, offset, to: send(flow, 3, full.at[field, rows], full.at[field, rows], to))

    def spread(flow):
        field, _, order = FLOWS[flow]
        arrived(flow, 3, 120)
        rows = pl.ds(pl.multiple_of(own(flow, 1), 8), 128)
        for shift in (2, 1, 3):
            send(flow, 4, full.at[field, rows], full.at[field, rows], device(order[0], shift))

    def share(flow):
        field = FLOWS[flow][0]
        arrived(flow, 4, 384)
        rows = pl.ds(pl.multiple_of(own(flow, 0), 8), 512)
        send(flow, 5, full.at[field, rows], full.at[field, rows], twin)

    def thrice(values):
        high, low = high_low(values)
        return jnp.concatenate([high, low, high], axis=0)

    def across_planes(source, target):
        for step in range(8):
            slices = [pl.ds(step * 4 + k, N, stride=32) for k in range(4)]
            values = jnp.concatenate([source[s, :] for s in slices], axis=1)
            values = jnp.dot(first[...], thrice(values), preferred_element_type=f32)
            values = values * jnp.concatenate([spectral[s, :] for s in slices], axis=1)
            values = jnp.dot(first[...], thrice(values), preferred_element_type=f32)
            for k in range(4):
                target[slices[k], :] = values[:, 128 * k:128 * k + 128]

    even = jnp.where(lax.broadcasted_iota(jnp.int32, (32, 1024), 1) % 128 < 64, 1.0, 0.0).astype(bf16)

    def within_planes(source, base, level=None):
        values = jnp.concatenate([source[pl.ds(base + 32 * k, 32), :] for k in range(8)], axis=1)
        if level is not None:
            values = values - level
        high, low = high_low(values)
        high0, low0 = high * even, low * even
        high1, low1 = high - high0, low - low0
        mixed = jnp.dot(second[...], jnp.concatenate([high0, high1, low0, low1, high0, high1], axis=0),
                        preferred_element_type=f32)
        high, low = high_low(jnp.concatenate([
            jnp.concatenate([mixed[0:32, 128 * k:128 * k + 128], mixed[32:64, 128 * k:128 * k + 128]], axis=1)
            for k in range(8)], axis=0))
        both = jnp.dot(high, third[...], preferred_element_type=f32)
        return both[:, 0:128] + (both[:, 128:256] + jnp.dot(low, third[:, 0:128], preferred_element_type=f32))

    def prepare():
        @pl.loop(0, 32)
        def planes(pair):
            for plane in (pair * 2, pair * 2 + 1):
                for component in range(4):
                    for block in range(4):
                        put(start, component, plane, block,
                            raw[pl.ds(plane * 128 + block * 32 + component, 8, stride=4), :])

    def opening_laplace(begin, end):
        upper = lax.broadcasted_iota(jnp.int32, (8, 128), 1) >= 64

        @pl.loop(begin, end)
        def groups(index):
            plane0 = index * GROUP
            beside_planes(start, near, beside, plane0)
            for sub in range(GROUP):
                plane = plane0 + sub
                for block in range(4):
                    rows = pl.ds(pl.multiple_of(plane * 32, 32) + 8 * block, 8)
                    for component in range(4):
                        laplace[component, rows, :] = neighbours(
                            start, beside, upper, plane, sub, component, 8 * block)[1]

    lead, rest = (0, 1), (2, 4, 3, 5)

    def each(flows, call, *levels):
        for flow in flows:
            call(flow, *levels)

    partial(0)
    partial(1)
    partial(2)
    add_core(0)
    partial(3)
    add_core(1)
    each(rest, add_core)
    prepare()
    for copy in tables_in:
        copy.wait()
    each(lead, lambda flow: arrived(flow, 1, 384))
    each(lead, add_line)
    opening_laplace(0, 2)
    for flow in rest:
        arrived(flow, 1, 384)
        add_line(flow)
    opening_laplace(2, 4)
    each(lead, add_layer)
    each(rest, add_layer)
    each(lead, spread)
    each(rest, spread)
    each(lead, share)
    mine = [pl.multiple_of(own(flow, 0) + part_row, 256) for flow in lead for part_row in (0, 256)]
    other = [pl.multiple_of(base + 512 - 1024 * core, 256) for base in mine]
    total = full[0, pl.ds(mine[0], 64), :]
    for base in mine:
        for row in range(0, 256, 64):
            if base is not mine[0] or row:
                total = total + full[0, pl.ds(base + row, 64), :]
    level = jnp.sum(total) * (1.0 / (1024 * 128))
    for base in mine:
        work[pl.ds(base, 256), :] = within_planes(full.at[0], base, level)
    each(lead, lambda flow: arrived(flow, 5, 512))
    for base in other:
        work[pl.ds(base, 256), :] = within_planes(full.at[0], base, level)
    each(rest, share)
    across_planes(work, hill)
    for step in range(8):
        rows = pl.ds(step * 256, 256)
        fields[0, rows, :] = 2.0 * (outer[rows, :] + full[0, rows, :] + within_planes(hill, step * 256)) + 6.0
    upper = lax.broadcasted_iota(jnp.int32, (8, 128), 1) >= 64

    def combine(plane, block, state, total, factor, store, held_fields=None):
        rows = pl.ds(pl.multiple_of(plane * 32, 32) + 8 * block, 8)
        mean, real, imag = held_fields or (fields[0, rows, :], fields[1, rows, :], fields[2, rows, :])
        a, b, c, d = state
        made = [mean * a - total[0] + (real * c - imag * d),
                mean * b - total[1] + (real * d + imag * c),
                (real * a + imag * b) - (mean * c - total[2]),
                (real * b - imag * a) - (mean * d - total[3])]
        old = [start[component, pl.ds(plane * PITCH + 8 + 8 * block, 8), :] for component in range(4)]
        half = 0.5 * factor
        store(plane, block, [old[0] + half * made[1], old[1] - half * made[0],
                             old[2] + half * made[3], old[3] - half * made[2]])

    def step(source, factor, store):
        def group(index):
            plane0 = index * GROUP
            beside_planes(source, near, beside, plane0)
            for sub in range(GROUP):
                for block in range(4):
                    both = [neighbours(source, beside, upper, plane0 + sub, sub, component, 8 * block)
                            for component in range(4)]
                    combine(plane0 + sub, block, [b[0] for b in both], [b[1] for b in both], factor, store)
        return group

    def into(state):
        def store(plane, block, values):
            for component in range(4):
                put(state, component, plane, block, values[component])
        return store

    def finish(plane, block, values):
        for component in range(4):
            raw[pl.ds(plane * 128 + block * 32 + component, 8, stride=4), :] = values[component]

    def opening(index):
        for sub in range(4):
            plane = index * 4 + sub
            for block in range(4):
                rows = pl.ds(pl.multiple_of(plane * 32, 32) + 8 * block, 8)
                scale = -2.0 * coupling[rows, :]
                real, imag = scale * full[1, rows, :], scale * full[2, rows, :]
                fields[1, rows, :] = real
                fields[2, rows, :] = imag
                state = [start[component, pl.ds(plane * PITCH + 8 + 8 * block, 8), :] for component in range(4)]
                total = [laplace[component, rows, :] for component in range(4)]
                combine(plane, block, state, total, time_step / 4, into(ping), (fields[0, rows, :], real, imag))

    for half in range(2):
        each(rest[2 * half:2 * half + 2], lambda flow: arrived(flow, 5, 512))
        pl.loop(half * 8, half * 8 + 8)(opening)
    held = pl.ds(lax.axis_index("grp") * 512 + lax.axis_index("wf"), 16, stride=32)
    potentials[0] = 0.5 * fields[0, held, :] - 3.0
    potentials[1] = 0.5 * fields[1, held, :]
    potentials[2] = 0.5 * fields[2, held, :]
    for source, degree, target in ((ping, 3, pong), (pong, 2, ping)):
        pl.loop(0, N // GROUP)(step(source, time_step / degree, into(target)))
    last = step(ping, time_step, finish)

    def save(index):
        rows = pl.ds(index * 2048, 2048)
        return pltpu.make_async_copy(raw.at[rows], out_hbm.at[rows], out_sem.at[index])

    @pl.loop(0, N // GROUP)
    def closing(index):
        last(index)
        save(index).start()

    for flow in lead + rest:
        for stage, rows in enumerate((512, 384, 120, 120, 384, 512)):
            whole(flow, stage, rows).wait_send()

    for index in range(N // GROUP):
        save(index).wait()

def copy_kernel(evolved_in, potentials_in, evolved, potentials, lines, small, in_sem, out_sem):
    pairs = [(evolved_in.at[rows], lines.at[rows], evolved.at[rows])
             for rows in (pl.ds(index * 512, 512) for index in range(16))]
    pairs.append((potentials_in, small, potentials))
    arrive = [pltpu.make_async_copy(a, b, in_sem.at[index]) for index, (a, b, _) in enumerate(pairs)]
    leave = [pltpu.make_async_copy(b, c, out_sem.at[index]) for index, (_, b, c) in enumerate(pairs)]
    for copy in arrive:
        copy.start()
    for come, go in zip(arrive, leave):
        come.wait()
        go.start()
    for copy in leave:
        copy.wait()


def local(quasi, outer_field, coupling):
    rows = quasi.reshape(4, ROWS, 128).transpose(1, 0, 2).reshape(4 * ROWS, 128)
    far = pl.BlockSpec(memory_space=pltpu.HBM)
    inside = pl.BlockSpec(memory_space=pltpu.VMEM)
    weights = [jnp.asarray(w) for w in tables()]
    shape = jax.ShapeDtypeStruct
    state = pltpu.VMEM((4, PADDED, 128), f32)
    field = pltpu.VMEM((ROWS, 128), f32)
    evolved, potentials = pl.pallas_call(
        kernel,
        out_shape=(shape((4 * ROWS, 128), f32), shape((3, 16, 128), f32)),
        in_specs=[far] * 8,
        out_specs=(far, inside),
        scratch_shapes=[
            pltpu.VMEM((4 * ROWS, 128), f32),
            pltpu.VMEM((3, ROWS, 128), f32),
            state,
            pltpu.VMEM((4, ROWS, 128), f32),
            state,
            state,
            pltpu.VMEM((3, ROWS, 128), f32),
            pltpu.VMEM((3, ROWS, 128), f32),
            pltpu.VMEM((6, 512, 128), f32),
            pltpu.VMEM((6, 384, 128), f32),
            pltpu.VMEM((6, 120, 128), f32),
            field,
            field,
        ] + [pltpu.VMEM(w.shape, w.dtype) for w in weights] + [
            field,
            field,
            pltpu.VMEM((GROUP * 128, 128), f32),
            pltpu.SemaphoreType.DMA((4,)),
            pltpu.SemaphoreType.DMA((6, 6)),
            pltpu.SemaphoreType.DMA((6, 6)),
            pltpu.SemaphoreType.DMA((7,)),
            pltpu.SemaphoreType.DMA((N // GROUP,)),
        ],
        compiler_params=pltpu.CompilerParams(
            collective_id=0, has_side_effects=True, vmem_limit_bytes=VMEM_MIB * 2**20),
        name="superfluid",
    )(rows, outer_field.reshape(ROWS, 128), coupling.reshape(ROWS, 128), *weights)
    evolved, potentials = pl.pallas_call(
        copy_kernel,
        out_shape=(shape((4 * ROWS, 128), f32), shape((3, 16, 128), f32)),
        in_specs=[far] * 2,
        out_specs=(far,) * 2,
        scratch_shapes=[
            pltpu.VMEM((4 * ROWS, 128), f32),
            pltpu.VMEM((3, 16, 128), f32),
            pltpu.SemaphoreType.DMA((17,)),
            pltpu.SemaphoreType.DMA((17,)),
        ],
        compiler_params=pltpu.CompilerParams(vmem_limit_bytes=VMEM_MIB * 2**20),
        name="deliver",
    )(evolved, potentials)
    evolved = evolved.reshape(ROWS, 4, 128).transpose(1, 0, 2).reshape(1, 4, ROWS * 128)
    return evolved, potentials


def solution(mesh):
    return jax.shard_map(
        local,
        mesh=mesh,
        in_specs=(P(("grp", "wf"), None, None), P(), P()),
        out_specs=(P(("grp", "wf"), None, None), P(None, "grp", "wf")),
        check_vma=False,
    )
```
